32 devices in a mesh: gx: 8 (over y, x, core), gy: 4 (over z).
Axes of the slice: x: 2, y: 2, z: 4, core: 2. Of those that a mesh axis runs over, the one named last changes fastest.
Arguments:
- fine_now: float32 [3, 64, 64, 128], P(None, 'gx', 'gy'), may hold values from -6 to 6
- fine_prev: float32 [3, 64, 64, 128], P(None, 'gx', 'gy'), may hold values from -6 to 6
- coarse_now: float32 [3, 32, 32, 128], P(None, 'gx', 'gy'), may hold values from -6 to 6
- coarse_prev: float32 [3, 32, 32, 128], P(None, 'gx', 'gy'), may hold values from -6 to 6
- fine_rho: float32 [64, 64, 128], P('gx', 'gy'), may hold values from 1 to 3
- fine_mu: float32 [64, 64, 128], P('gx', 'gy'), may hold values from 0.3 to 1.5
- fine_lam: float32 [64, 64, 128], P('gx', 'gy'), may hold values from 0.3 to 1.5
- fine_metric: float32 [64, 64, 128], P('gx', 'gy'), may hold values from 0.5 to 2
- coarse_rho: float32 [32, 32, 128], P('gx', 'gy'), may hold values from 1 to 3
- coarse_mu: float32 [32, 32, 128], P('gx', 'gy'), may hold values from 0.3 to 1.5
- coarse_lam: float32 [32, 32, 128], P('gx', 'gy'), may hold values from 0.3 to 1.5
- coarse_metric: float32 [32, 32, 128], P('gx', 'gy'), may hold values from 0.5 to 2
- couple_index: int32 [64, 64, 16], P('gx', 'gy'), may hold values from 0 to 95, as said below
- couple_weight: float32 [64, 64, 16], P('gx', 'gy'), may hold values from 0 to 0.125
Outputs:
- fine_field: float32 [3, 64, 64, 128], P(None, 'gx', 'gy')
- coarse_field: float32 [3, 32, 32, 128], P(None, 'gx', 'gy')
The draws below stay inside these ranges and needn't reach their ends.
Inputs may be any that keep to these rules, and one draw needn't show every extreme that they name: `couple_index`: the sixteen indices of a fine point are a 4 x 4 patch of neighbouring coarse cells of its block's widened top plane, lying within 2 coarse cells of the point's own coarse cell.
All inputs are finite; a program needn't handle non-finite values.
Results may differ from the reference program's by a relative error of at most 0.0001.
Values sent between devices are 32-bit elements; how exact they have to be, the bound alone decides.
A program may use at most 64 MiB of HBM per device.

```python
import math
import jax
import jax.numpy as jnp
import numpy as np
from jax import lax

CXF = 8
CYF = 16
NZ = 128
COUPLE = 16
CXC = 4
CYC = 8
NXF = 64
NYF = 64
NXC = 32
NYC = 32


def draw_couple_index(key, part):
    key_row, key_col = jax.random.split(key)
    row_local = jnp.arange(NXF, dtype=jnp.int32) % CXF
    col_local = jnp.arange(NYF, dtype=jnp.int32) % CYF
    shift_row = jax.random.randint(key_row, (NXF, NYF), -1, 1, dtype=jnp.int32)
    shift_col = jax.random.randint(key_col, (NXF, NYF), -1, 1, dtype=jnp.int32)
    shift_row = jnp.where(row_local[:, None] == 0, -1, jnp.where(row_local[:, None] == CXF - 1, 0, shift_row))
    shift_col = jnp.where(col_local[None, :] == 0, -1, jnp.where(col_local[None, :] == CYF - 1, 0, shift_col))
    base_row = row_local[:, None] // 2 + 1 + shift_row
    base_col = col_local[None, :] // 2 + 1 + shift_col
    spread = jnp.arange(4, dtype=jnp.int32)
    grid_row = base_row[:, :, None, None] + spread[None, None, :, None]
    grid_col = base_col[:, :, None, None] + spread[None, None, None, :]
    return (grid_row * (CYC + 4) + grid_col).reshape(NXF, NYF, COUPLE).astype(jnp.int32)


def steps_of(stream_key, dims, pieces, least, high):
    def one(position, shards_of):
        heights = jax.random.uniform(jax.random.fold_in(jax.random.fold_in(stream_key, 6), position), (shards_of,), jnp.float32, least / len(pieces), high / len(pieces))
        return jnp.repeat(jnp.exp(heights), dims[position] // shards_of).reshape((-1,) + (1,) * (len(dims) - position - 1))

    factor_of = one(*pieces[0])
    for cut in pieces[1:]:
        factor_of = factor_of * one(*cut)
    return factor_of


def gaussian(stream_key, shape, scale, bound, shards=(), kind=jnp.bfloat16):
    gain = steps_of(stream_key, shape, shards, -0.22, 0.18) if shards else 1.0
    result = jax.random.normal(stream_key, shape, jnp.float32) * scale * gain
    return jnp.minimum(jnp.maximum(result, -bound), bound).astype(kind)


def setup_inputs(seed: int = 0) -> dict:
    arg_keys = jax.random.split(jax.random.key(seed), 15)
    return {
        "fine_now": gaussian(arg_keys[0], (3, NXF, NYF, NZ), 1.0, 6.0, ((1, 8), (2, 4)), jnp.float32),
        "fine_prev": gaussian(arg_keys[1], (3, NXF, NYF, NZ), 1.0, 6.0, ((1, 8), (2, 4)), jnp.float32),
        "coarse_now": gaussian(arg_keys[2], (3, NXC, NYC, NZ), 1.0, 6.0, ((1, 8), (2, 4)), jnp.float32),
        "coarse_prev": gaussian(arg_keys[3], (3, NXC, NYC, NZ), 1.0, 6.0, ((1, 8), (2, 4)), jnp.float32),
        "fine_rho": jnp.clip(jnp.exp(math.log(3.0) - 1.0986123 * jax.random.uniform(arg_keys[4], (NXF, NYF, NZ), jnp.float32) ** steps_of(arg_keys[4], (NXF, NYF, NZ), ((0, 8), (1, 4)), -0.2, 0.2)), 1.0, 3.0),
        "fine_mu": jnp.clip(jnp.exp(math.log(1.5) - 1.60943787 * jax.random.uniform(arg_keys[5], (NXF, NYF, NZ), jnp.float32) ** steps_of(arg_keys[5], (NXF, NYF, NZ), ((0, 8), (1, 4)), -0.2, 0.2)), 0.3, 1.5),
        "fine_lam": jnp.clip(jnp.exp(math.log(1.5) - 1.60943787 * jax.random.uniform(arg_keys[6], (NXF, NYF, NZ), jnp.float32) ** steps_of(arg_keys[6], (NXF, NYF, NZ), ((0, 8), (1, 4)), -0.2, 0.2)), 0.3, 1.5),
        "fine_metric": jnp.clip(jnp.exp(math.log(2.0) - 1.3862944 * jax.random.uniform(arg_keys[7], (NXF, NYF, NZ), jnp.float32) ** steps_of(arg_keys[7], (NXF, NYF, NZ), ((0, 8), (1, 4)), -0.2, 0.2)), 0.5, 2.0),
        "coarse_rho": jnp.clip(jnp.exp(math.log(3.0) - 1.0986123 * jax.random.uniform(arg_keys[8], (NXC, NYC, NZ), jnp.float32) ** steps_of(arg_keys[8], (NXC, NYC, NZ), ((0, 8), (1, 4)), -0.2, 0.2)), 1.0, 3.0),
        "coarse_mu": jnp.clip(jnp.exp(math.log(1.5) - 1.60943787 * jax.random.uniform(arg_keys[9], (NXC, NYC, NZ), jnp.float32) ** steps_of(arg_keys[9], (NXC, NYC, NZ), ((0, 8), (1, 4)), -0.2, 0.2)), 0.3, 1.5),
        "coarse_lam": jnp.clip(jnp.exp(math.log(1.5) - 1.60943787 * jax.random.uniform(arg_keys[10], (NXC, NYC, NZ), jnp.float32) ** steps_of(arg_keys[10], (NXC, NYC, NZ), ((0, 8), (1, 4)), -0.2, 0.2)), 0.3, 1.5),
        "coarse_metric": jnp.clip(jnp.exp(math.log(2.0) - 1.3862944 * jax.random.uniform(arg_keys[11], (NXC, NYC, NZ), jnp.float32) ** steps_of(arg_keys[11], (NXC, NYC, NZ), ((0, 8), (1, 4)), -0.2, 0.2)), 0.5, 2.0),
        "couple_index": draw_couple_index(jax.random.fold_in(arg_keys[14], 71), 0),
        "couple_weight": jnp.clip(0.125 * jax.random.uniform(arg_keys[13], (NXF, NYF, COUPLE), jnp.float32) ** steps_of(arg_keys[13], (NXF, NYF, COUPLE), ((0, 8), (1, 4)), -0.2, 0.2), 0.0, 0.125),
    }


time_step = 0.25


def vertical_table(layers):
    matrix = np.zeros((layers, layers))
    for centre in range(2, layers - 2):
        matrix[centre, centre - 2] = 1.0 / 12.0
        matrix[centre, centre - 1] = -8.0 / 12.0
        matrix[centre, centre + 1] = 8.0 / 12.0
        matrix[centre, centre + 2] = -1.0 / 12.0
    matrix[0, 0] = -1.5
    matrix[0, 1] = 2.0
    matrix[0, 2] = -0.5
    matrix[1, 0] = -0.5
    matrix[1, 2] = 0.5
    matrix[layers - 2, layers - 3] = -0.5
    matrix[layers - 2, layers - 1] = 0.5
    matrix[layers - 1, layers - 3] = 0.5
    matrix[layers - 1, layers - 2] = -2.0
    matrix[layers - 1, layers - 1] = 1.5
    return jnp.asarray(matrix.T, jnp.float32)


def vertical(values, depth_table):
    return jnp.matmul(values, depth_table, precision=lax.Precision.HIGHEST)


def stencil_sum(source, along, weights):
    extent = source.shape[along] - 4
    running = None
    for offset in range(5):
        if weights[offset] != 0.0:
            contrib = weights[offset] * lax.slice_in_dim(source, offset, offset + extent, axis=along)
            running = contrib if running is None else running + contrib
    return running


def advance(widened, lifted, present, earlier, metric, density, shear, lame_first, depth_table, spacing):
    first_taps = [c / (12.0 * spacing) for c in (1.0, -8.0, 0.0, 8.0, -1.0)]
    second_taps = [c / (12.0 * spacing * spacing) for c in (-1.0, 16.0, -30.0, 16.0, -1.0)]
    curve_x = stencil_sum(widened[:, :, 2:-2], 1, second_taps)
    curve_y = stencil_sum(widened[:, 2:-2], 2, second_taps)
    cross_one = stencil_sum(stencil_sum(widened[1], 1, first_taps), 0, first_taps)
    cross_zero = stencil_sum(stencil_sum(widened[0], 0, first_taps), 1, first_taps)
    lifted_dx = stencil_sum(lifted[:, 2:-2], 0, first_taps)
    lifted_dy = stencil_sum(lifted[2:-2], 1, first_taps)
    along_x = stencil_sum(widened[0, :, 2:-2], 0, first_taps)
    along_y = stencil_sum(widened[1, 2:-2], 1, first_taps)
    lifted_in = lifted[2:-2, 2:-2]
    slopes = metric * vertical(present[0:2], depth_table)
    stacked = jnp.concatenate([slopes, lifted_in[None], (along_x + along_y + lifted_in)[None]], 0)
    bent_terms = metric * vertical(stacked, depth_table)
    laplace = curve_x + curve_y + bent_terms[0:3]
    grad_div = jnp.stack([curve_x[0] + cross_one + lifted_dx, cross_zero + curve_y[1] + lifted_dy, bent_terms[3]], 0)
    acceleration = (shear * laplace + (lame_first + shear) * grad_div) / density
    return 2.0 * present - earlier + (time_step * time_step) * acceleration


def interpolate(flat_plane, targets, mixing):
    return jnp.sum(flat_plane[:, targets] * mixing, axis=-1)


def reference(fine_now, fine_prev, coarse_now, coarse_prev, fine_rho, fine_mu, fine_lam, fine_metric, coarse_rho, coarse_mu, coarse_lam, coarse_metric, couple_index, couple_weight):
    depth_table = vertical_table(NZ)
    margin_pad = ((2, 2), (2, 2), (0, 0))
    fine_edge = jnp.pad(fine_metric, margin_pad)
    coarse_edge = jnp.pad(coarse_metric, margin_pad)
    row_start = jnp.arange(NXF, dtype=jnp.int32) // CXF * CXC
    col_start = jnp.arange(NYF, dtype=jnp.int32) // CYF * CYC
    global_row = row_start[:, None, None] + couple_index // (CYC + 4)
    global_col = col_start[None, :, None] + couple_index % (CYC + 4)
    flat_index = (global_row * (NYC + 4) + global_col).astype(jnp.int32)
    for marching in range(2):
        fine_wide = jnp.pad(fine_now, ((0, 0),) + margin_pad)
        fine_lift = fine_edge * vertical(fine_wide[2], depth_table)
        fine_next = advance(fine_wide, fine_lift, fine_now, fine_prev, fine_metric, fine_rho, fine_mu, fine_lam, depth_table, 1.0)
        coarse_wide = jnp.pad(coarse_now, ((0, 0),) + margin_pad)
        coarse_lift = coarse_edge * vertical(coarse_wide[2], depth_table)
        coarse_next = advance(coarse_wide, coarse_lift, coarse_now, coarse_prev, coarse_metric, coarse_rho, coarse_mu, coarse_lam, depth_table, 2.0)
        top_plane = jnp.pad(coarse_next[:, :, :, NZ - 1], ((0, 0), (2, 2), (2, 2)))
        interface_values = interpolate(top_plane.reshape(3, -1), flat_index, couple_weight)
        fine_next = fine_next.at[:, :, :, 0].set(interface_values)
        fine_prev, fine_now = fine_now, fine_next
        coarse_prev, coarse_now = coarse_now, coarse_next
    return (fine_now, coarse_now)
```

```python
import functools

import jax
import jax.numpy as jnp
from jax import lax
from jax.experimental import pallas as pl
from jax.experimental.pallas import tpu as pltpu
from jax.sharding import PartitionSpec as P

MESH = pl.DeviceIdType.MESH
f32 = jnp.float32
bf16 = jnp.bfloat16
time_step = 0.25
OFF = 8
SIDES = ((-1, 0), (1, 0), (0, -1), (0, 1))
CORNERS = ((-1, -1), (-1, 1), (1, -1), (1, 1))
DIRS = SIDES + CORNERS


def vertical_table12(layers):
    level_in = lax.broadcasted_iota(jnp.int32, (layers, layers), 0)
    level_out = lax.broadcasted_iota(jnp.int32, (layers, layers), 1)
    apart = level_in - level_out
    table = jnp.where(apart == -2, 1.0, 0.0)
    table = jnp.where(apart == -1, -8.0, table)
    table = jnp.where(apart == 1, 8.0, table)
    table = jnp.where(apart == 2, -1.0, table)
    last = layers - 1
    edges = {
        0: ((0, -18.0), (1, 24.0), (2, -6.0)),
        1: ((0, -6.0), (2, 6.0)),
        last - 1: ((last - 2, -6.0), (last, 6.0)),
        last: ((last - 2, 6.0), (last - 1, -24.0), (last, 18.0)),
    }
    for row, taps in edges.items():
        column = jnp.zeros_like(table)
        for level, value in taps:
            column = jnp.where(level_in == level, value, column)
        table = jnp.where(level_out == row, column, table)
    return table.astype(bf16)


def halves(values):
    high = values.astype(bf16)
    low = (values - high.astype(f32)).astype(bf16)
    return high, low


def dot(left, right):
    return jnp.dot(left, right, preferred_element_type=f32)


def vertical12(values, table2):
    shape = values.shape
    high, low = halves(values.reshape(-1, shape[-1]))
    return dot(jnp.concatenate([high, low], axis=1), table2).reshape(shape)


def advance(u, metric, lift, bend, earlier, shear, both, table2, nx, ny, spacing):
    inner_x, inner_y = slice(2, 2 + nx), slice(OFF, OFF + ny)
    t1 = 1.0 / (12.0 * spacing)
    t2 = 1.0 / (12.0 * spacing * spacing)

    def first(m2, m1, p1, p2):
        return t1 * ((m2 - p2) + 8.0 * (p1 - m1))

    def second(m2, m1, mid, p1, p2):
        return t2 * (16.0 * (m1 + p1) - (m2 + p2) - 30.0 * mid)

    def along_y(read):
        return [read(slice(OFF + s, OFF + s + ny)) for s in (-2, -1, 0, 1, 2)]

    def along_x(values):
        return [values[2 + s : 2 + s + nx] for s in (-2, -1, 0, 1, 2)]

    metric_wide = metric[...] * (1.0 / 12.0)
    metric_in = metric_wide[inner_x, inner_y]
    lift[...] = metric_wide * vertical12(u[2], table2)
    lifted_in = lift[inner_x, inner_y]

    m2, m1, mid, p1, p2 = along_y(lambda ys: u[1, :, ys])
    slant = first(m2, m1, p1, p2) + lift[:, inner_y]
    curve_y1 = second(*[v[inner_x] for v in (m2, m1, mid, p1, p2)])
    curve_x1 = second(*along_x(mid))
    m2, m1, _, p1, p2 = along_x(slant)
    graddiv_0 = first(m2, m1, p1, p2)

    m2, m1, mid, p1, p2 = along_x(u[0])
    bend[...] = first(m2, m1, p1, p2) + lift[inner_x]
    curve_x0 = second(*[v[:, inner_y] for v in (m2, m1, mid, p1, p2)])
    curve_y0 = second(*along_y(lambda ys: u[0, inner_x, ys]))
    m2, m1, mid, p1, p2 = along_y(lambda ys: bend[:, ys])
    graddiv_1 = first(m2, m1, p1, p2)

    spread = slant[inner_x] + mid - lifted_in
    present = u[0:3, inner_x, inner_y]
    slopes = metric_in * vertical12(present[0:2], table2)
    stacked = jnp.concatenate([slopes, lifted_in[None], spread[None]], axis=0)
    bent = metric_in * vertical12(stacked, table2)

    curve_2 = second(*along_x(u[2, :, inner_y])) + second(*along_y(lambda ys: u[2, inner_x, ys]))
    laplace = (curve_x0 + curve_y0 + bent[0], curve_x1 + curve_y1 + bent[1], curve_2 + bent[2])
    graddiv = (curve_x0 + graddiv_0, curve_y1 + graddiv_1, bent[3])
    return [
        2.0 * present[c] - earlier(c) + (shear * laplace[c] + both * graddiv[c]) for c in range(3)
    ]


def kernel(
    size_x,
    size_y,
    fine_now,
    fine_prev,
    coarse_now,
    coarse_prev,
    fine_rho,
    fine_mu,
    fine_lam,
    fine_metric,
    coarse_rho,
    coarse_mu,
    coarse_lam,
    coarse_metric,
    couple_index,
    couple_weight,
    fine_out,
    coarse_out,
    f1,
    f2,
    c1,
    c2,
    f_old,
    c_old,
    f_par,
    c_par,
    index_in,
    weight_in,
    f_lift,
    f_bend,
    c_lift,
    c_bend,
    t1,
    t2,
    mix,
    table,
    f_last,
    c_last,
    load_sem,
    out_sem,
    send_sem,
    recv_sem,
):
    nxf, nyf, layers = fine_rho.shape
    nxc, nyc, _ = coarse_rho.shape
    span = OFF + nyc
    gx, gy = lax.axis_index("gx"), lax.axis_index("gy")

    def inner(nx, ny):
        return pl.ds(2, nx), pl.ds(OFF, ny)

    fx, fy = inner(nxf, nyf)
    cx, cy = inner(nxc, nyc)
    pairs = [
        (coarse_now, c1.at[0:3, cx, cy]),
        (coarse_metric, c1.at[3, cx, cy]),
        (fine_now, f1.at[0:3, fx, fy]),
        (fine_metric, f1.at[3, fx, fy]),
        (couple_index, index_in),
        (couple_weight, weight_in),
        (coarse_rho, c_par.at[0]),
        (coarse_mu, c_par.at[1]),
        (coarse_lam, c_par.at[2]),
        (coarse_prev, c_old),
        (fine_rho, f_par.at[0]),
        (fine_mu, f_par.at[1]),
        (fine_lam, f_par.at[2]),
        (fine_prev, f_old),
    ]
    loads = [
        pltpu.make_async_copy(source, target, load_sem.at[n])
        for n, (source, target) in enumerate(pairs)
    ]
    for load in loads:
        load.start()

    def exists(dx, dy):
        ok = None
        for step, position, size in ((dx, gx, size_x), (dy, gy, size_y)):
            if step:
                here = position >= 1 if step < 0 else position <= size - 2
                ok = here if ok is None else jnp.logical_and(ok, here)
        return ok

    barrier = pltpu.get_barrier_semaphore()
    for dx, dy in DIRS:

        @pl.when(exists(dx, dy))
        def _():
            pl.semaphore_signal(
                barrier, inc=1, device_id=(gx + dx, gy + dy), device_id_type=MESH
            )

    def source_range(step, start, length):
        return {-1: pl.ds(start, 2), 1: pl.ds(start + length - 2, 2), 0: pl.ds(start, length)}[step]

    def target_range(step, start, length, wrap=0):
        after = start + length - wrap
        return {-1: pl.ds(after, 2), 1: pl.ds(start - 2, 2), 0: pl.ds(start, length)}[step]

    class Exchange:
        def __init__(self, base, buffer, nx, ny, sides, corners, wrap=0):
            self.copies = []
            self.targets = []
            for n, (dx, dy) in enumerate(DIRS):
                parts = sides if n < 4 else corners
                xs, ys = source_range(dx, 2, nx), source_range(dy, OFF, ny)
                xt, yt = target_range(dx, 2, nx), target_range(dy, OFF, ny, wrap)
                if parts is None:
                    src, dst = buffer.at[xs, ys], buffer.at[xt, yt]
                    self.targets.append((buffer, (xt, yt), (xt.size, yt.size, layers)))
                else:
                    ps = pl.ds(0, parts)
                    src, dst = buffer.at[ps, xs, ys], buffer.at[ps, xt, yt]
                    self.targets.append((buffer, (ps, xt, yt), (parts, xt.size, yt.size, layers)))
                copy = pltpu.make_async_remote_copy(
                    src_ref=src,
                    dst_ref=dst,
                    send_sem=send_sem.at[base + n],
                    recv_sem=recv_sem.at[base + n],
                    device_id=(gx + dx, gy + dy),
                    device_id_type=MESH,
                )
                self.copies.append(copy)

        def start(self):
            for (dx, dy), copy in zip(DIRS, self.copies):
                pl.when(exists(dx, dy))(copy.start)

        def arrive(self):
            for (dx, dy), copy in zip(DIRS, self.copies):
                pl.when(exists(-dx, -dy))(copy.wait_recv)

        def finish(self):
            for (dx, dy), copy in zip(DIRS, self.copies):
                pl.when(exists(dx, dy))(copy.wait_send)

    coarse_a = Exchange(0, c1, nxc, nyc, 4, 2)
    fine_a = Exchange(8, f1, nxf, nyf, 4, 2)
    coarse_b = Exchange(16, c2, nxc, nyc, 3, 3)
    fine_b = Exchange(24, f2, nxf, nyf, 3, 2)
    top_c = Exchange(32, t2, nxc, nyc, None, None, wrap=span)
    exchanges = (coarse_a, fine_a, coarse_b, fine_b, top_c)

    for load in loads[0:4]:
        load.wait()
    sides_x = 1 + (gx >= 1).astype(jnp.int32) + (gx <= size_x - 2).astype(jnp.int32)
    sides_y = 1 + (gy >= 1).astype(jnp.int32) + (gy <= size_y - 2).astype(jnp.int32)
    pl.semaphore_wait(barrier, sides_x * sides_y - 1)
    coarse_a.start()
    fine_a.start()

    for n, (dx, dy) in enumerate(DIRS):

        @pl.when(jnp.logical_not(exists(-dx, -dy)))
        def _():
            for exchange in exchanges:
                buffer, where, shape = exchange.targets[n]
                buffer[where] = jnp.zeros(shape, f32)

    half = vertical_table12(layers)
    table[...] = jnp.concatenate([half, half], axis=0)

    for load in loads[4:6]:
        load.wait()
    width = nyc + 4
    reciprocal = (2048 + width - 1) // width
    cells = (nxc + 4) * span
    index = index_in[...].reshape(nxf * nyf, -1)
    weight = weight_in[...].reshape(nxf * nyf, -1)
    row = jnp.right_shift(index * reciprocal, 11)
    column = index - row * width + (OFF - 2)
    column = jnp.where(column >= span, column - span, column)
    place = row * span + column
    cell = lax.broadcasted_iota(jnp.int32, (nxf * nyf, cells), 1)
    total = jnp.zeros((nxf * nyf, cells), f32)
    for j in range(index.shape[1]):
        total += jnp.where(cell == place[:, j : j + 1], weight[:, j : j + 1], 0.0)
    mix_high, mix_low = halves(total)
    mix[0] = mix_high
    mix[1] = mix_low

    for load in loads[6:]:
        load.wait()
    for par in (c_par, f_par):
        scale = (time_step * time_step) / par[0]
        shear = par[1]
        par[0] = shear * scale
        par[1] = (par[2] + shear) * scale

    lane = lax.broadcasted_iota(jnp.int32, (1, 1, layers), 2)

    def tops(parts):
        out = None
        for c, values in enumerate(parts):
            only = jnp.where(lane == layers - 1, values, 0.0)
            moved = pltpu.roll(only.reshape(-1, layers), c + 1, 1).reshape(values.shape)
            out = moved if out is None else out + moved
        return out

    def interface(top, parts):
        high, low = halves(top[...].reshape(cells, layers))
        found = dot(mix[0], high) + (dot(mix[1], high) + dot(mix[0], low))
        result = []
        for c, values in enumerate(parts):
            moved = found if c == 0 else pltpu.roll(found, layers - c, 1)
            result.append(jnp.where(lane == 0, moved.reshape(values.shape), values))
        return result

    f_in = (slice(2, 2 + nxf), slice(OFF, OFF + nyf))
    c_in = (slice(2, 2 + nxc), slice(OFF, OFF + nyc))

    def fine_step(u, earlier):
        return advance(
            u, f1.at[3], f_lift, f_bend, earlier, f_par[0], f_par[1], table[...], nxf, nyf, 1.0
        )

    def coarse_step(u, earlier):
        return advance(
            u, c1.at[3], c_lift, c_bend, earlier, c_par[0], c_par[1], table[...], nxc, nyc, 2.0
        )

    coarse_a.arrive()
    for c, values in enumerate(coarse_step(c1, lambda c: c_old[c])):
        c2[c, c_in[0], c_in[1]] = values
    coarse_b.start()
    fine_a.arrive()
    fine_next = fine_step(f1, lambda c: f_old[c])
    for c, values in enumerate(fine_next):
        f_last[c] = values
    coarse_b.arrive()
    sub = lax.broadcasted_iota(jnp.int32, (1, OFF, 1), 1)
    rims = []
    for c in range(3):
        after, before = c2[c, :, OFF + nyc : 2 * OFF + nyc], c2[c, :, 0:OFF]
        rims.append(jnp.where(sub < 2, after, jnp.where(sub >= OFF - 2, before, 0.0)))
    t1[:, 0:OFF] = tops(rims)
    t1[:, OFF:span] = tops([c2[c, :, c_in[1]] for c in range(3)])
    for c, values in enumerate(interface(t1, [f_last[c] for c in range(3)])):
        f2[c, f_in[0], f_in[1]] = values
    fine_b.start()

    coarse_next = coarse_step(c2, lambda c: c1[c, c_in[0], c_in[1]])
    for c, values in enumerate(coarse_next):
        c_last[c] = values
    t2[c_in[0], c_in[1]] = tops(coarse_next)
    top_c.start()
    store_coarse = pltpu.make_async_copy(c_last, coarse_out, out_sem.at[0])
    store_coarse.start()
    fine_b.arrive()
    fine_next = fine_step(f2, lambda c: f1[c, f_in[0], f_in[1]])
    for c, values in enumerate(fine_next):
        f_last[c] = values
    top_c.arrive()
    blank = t2[:, 0:OFF]
    t2_rim = jnp.where(jnp.logical_or(sub < 2, sub >= OFF - 2), blank, 0.0)
    top = jnp.concatenate([t2_rim, t2[:, OFF:span]], axis=1)
    for c, values in enumerate(interface(top, [f_last[c] for c in range(3)])):
        f_last[c] = values
    store_fine = pltpu.make_async_copy(f_last, fine_out, out_sem.at[1])
    store_fine.start()
    for exchange in exchanges:
        exchange.finish()
    store_coarse.wait()
    store_fine.wait()


def solution(mesh):
    size_x, size_y = mesh.shape["gx"], mesh.shape["gy"]

    def on_device(*args):
        fine, coarse = args[0], args[2]
        _, nxf, nyf, layers = fine.shape
        _, nxc, nyc, _ = coarse.shape
        index = args[12]

        def wide(parts, nx, ny):
            return pltpu.VMEM((parts, nx + 4, ny + 2 * OFF, layers), f32)

        span = OFF + nyc
        scratch = [
            wide(4, nxf, nyf),
            wide(3, nxf, nyf),
            wide(4, nxc, nyc),
            wide(3, nxc, nyc),
            pltpu.VMEM(fine.shape, f32),
            pltpu.VMEM(coarse.shape, f32),
            pltpu.VMEM(fine.shape, f32),
            pltpu.VMEM(coarse.shape, f32),
            pltpu.VMEM(index.shape, jnp.int32),
            pltpu.VMEM(index.shape, f32),
            pltpu.VMEM((nxf + 4, nyf + 2 * OFF, layers), f32),
            pltpu.VMEM((nxf, nyf + 2 * OFF, layers), f32),
            pltpu.VMEM((nxc + 4, nyc + 2 * OFF, layers), f32),
            pltpu.VMEM((nxc, nyc + 2 * OFF, layers), f32),
            pltpu.VMEM((nxc + 4, span, layers), f32),
            pltpu.VMEM((nxc + 4, span, layers), f32),
            pltpu.VMEM((2, nxf * nyf, (nxc + 4) * span), bf16),
            pltpu.VMEM((2 * layers, layers), bf16),
            pltpu.VMEM(fine.shape, f32),
            pltpu.VMEM(coarse.shape, f32),
            pltpu.SemaphoreType.DMA((14,)),
            pltpu.SemaphoreType.DMA((2,)),
            pltpu.SemaphoreType.DMA((40,)),
            pltpu.SemaphoreType.DMA((40,)),
        ]
        return pl.pallas_call(
            functools.partial(kernel, size_x, size_y),
            out_shape=(
                jax.ShapeDtypeStruct(fine.shape, f32),
                jax.ShapeDtypeStruct(coarse.shape, f32),
            ),
            in_specs=[pl.BlockSpec(memory_space=pl.ANY)] * 14,
            out_specs=(pl.BlockSpec(memory_space=pl.ANY), pl.BlockSpec(memory_space=pl.ANY)),
            scratch_shapes=scratch,
            compiler_params=pltpu.CompilerParams(
                collective_id=0, has_side_effects=True, vmem_limit_bytes=32 * 1024 * 1024
            ),
        )(*args)

    field, flat = P(None, "gx", "gy", None), P("gx", "gy", None)
    return jax.shard_map(
        on_device,
        mesh=mesh,
        in_specs=(field,) * 4 + (flat,) * 10,
        out_specs=(field, field),
        check_vma=False,
    )
```

```python
import functools

import jax
import jax.numpy as jnp
from jax import lax
from jax.experimental import pallas as pl
from jax.experimental.pallas import tpu as pltpu
from jax.sharding import PartitionSpec as P

MESH = pl.DeviceIdType.MESH
f32 = jnp.float32
bf16 = jnp.bfloat16
time_step = 0.25
OFF = 8
SIDES = ((-1, 0), (1, 0), (0, -1), (0, 1))
CORNERS = ((-1, -1), (-1, 1), (1, -1), (1, 1))
DIRS = SIDES + CORNERS


def vertical_table12(layers):
    level_in = lax.broadcasted_iota(jnp.int32, (layers, layers), 0)
    level_out = lax.broadcasted_iota(jnp.int32, (layers, layers), 1)
    apart = level_in - level_out
    table = jnp.where(apart == -2, 1.0, 0.0)
    table = jnp.where(apart == -1, -8.0, table)
    table = jnp.where(apart == 1, 8.0, table)
    table = jnp.where(apart == 2, -1.0, table)
    last = layers - 1
    edges = {
        0: ((0, -18.0), (1, 24.0), (2, -6.0)),
        1: ((0, -6.0), (2, 6.0)),
        last - 1: ((last - 2, -6.0), (last, 6.0)),
        last: ((last - 2, 6.0), (last - 1, -24.0), (last, 18.0)),
    }
    for row, taps in edges.items():
        column = jnp.zeros_like(table)
        for level, value in taps:
            column = jnp.where(level_in == level, value, column)
        table = jnp.where(level_out == row, column, table)
    return table.astype(bf16)


def halves(values):
    high = values.astype(bf16)
    low = (values - high.astype(f32)).astype(bf16)
    return high, low


def dot(left, right):
    return jnp.dot(left, right, preferred_element_type=f32)


def vertical12(values, table2):
    shape = values.shape
    high, low = halves(values.reshape(-1, shape[-1]))
    return dot(jnp.concatenate([high, low], axis=1), table2).reshape(shape)


def before_halo(u, metric, lift, base, earlier, shear, table2, nx, ny):
    inner_x, inner_y = slice(2, 2 + nx), slice(OFF, OFF + ny)
    metric_in = metric[inner_x, inner_y] * (1.0 / 12.0)
    present = u[0:3, inner_x, inner_y]
    slopes = metric_in * vertical12(present, table2)
    lift[inner_x, inner_y] = slopes[2]
    bent = metric_in * vertical12(slopes, table2)
    for c in range(3):
        base[c] = 2.0 * present[c] - earlier(c) + shear * bent[c]


def after_halo(u, metric, lift, bend, base, shear, both, table2, nx, ny, spacing, put):
    inner_x, inner_y = slice(2, 2 + nx), slice(OFF, OFF + ny)
    t1 = 1.0 / (12.0 * spacing)
    t2 = 1.0 / (12.0 * spacing * spacing)

    def first(m2, m1, p1, p2):
        return t1 * ((m2 - p2) + 8.0 * (p1 - m1))

    def second(m2, m1, mid, p1, p2):
        return t2 * (16.0 * (m1 + p1) - (m2 + p2) - 30.0 * mid)

    def along_y(read):
        return [read(slice(OFF + s, OFF + s + ny)) for s in (-2, -1, 0, 1, 2)]

    def along_x(values):
        return [values[2 + s : 2 + s + nx] for s in (-2, -1, 0, 1, 2)]

    layers = u.shape[-1]
    rims = (
        (slice(0, 2), inner_y),
        (slice(2 + nx, 4 + nx), inner_y),
        (inner_x, slice(0, OFF)),
        (inner_x, slice(OFF + ny, 2 * OFF + ny)),
    )
    rows = [u[2, xs, ys].reshape(-1, layers) for xs, ys in rims]
    found = vertical12(jnp.concatenate(rows, axis=0), table2)
    start = 0
    for (xs, ys), part in zip(rims, rows):
        scale = metric[xs, ys] * (1.0 / 12.0)
        lift[xs, ys] = scale * found[start : start + part.shape[0]].reshape(scale.shape)
        start += part.shape[0]

    m2, m1, mid, p1, p2 = along_x(u[0])
    bend[...] = first(m2, m1, p1, p2) + lift[inner_x]
    curve_x0 = second(*[v[:, inner_y] for v in (m2, m1, mid, p1, p2)])
    slope_x0 = bend[:, inner_y]

    m2, m1, mid, p1, p2 = along_y(lambda ys: u[1, :, ys])
    slant = first(m2, m1, p1, p2) + lift[:, inner_y]
    spread = slant[inner_x] + slope_x0 - lift[inner_x, inner_y]
    bent = (metric[inner_x, inner_y] * (1.0 / 12.0)) * vertical12(spread, table2)
    curve_y1 = second(*[v[inner_x] for v in (m2, m1, mid, p1, p2)])
    curve_x1 = second(*along_x(mid))
    m2, m1, _, p1, p2 = along_x(slant)
    graddiv_0 = curve_x0 + first(m2, m1, p1, p2)
    curve_y0 = second(*along_y(lambda ys: u[0, inner_x, ys]))
    put(0, base[0] + shear * (curve_x0 + curve_y0) + both * graddiv_0)

    m2, m1, mid, p1, p2 = along_y(lambda ys: bend[:, ys])
    graddiv_1 = curve_y1 + first(m2, m1, p1, p2)
    put(1, base[1] + shear * (curve_x1 + curve_y1) + both * graddiv_1)

    curve_2 = second(*along_x(u[2, :, inner_y])) + second(*along_y(lambda ys: u[2, inner_x, ys]))
    put(2, base[2] + shear * curve_2 + both * bent)


def kernel(
    size_x,
    size_y,
    fine_now,
    fine_prev,
    coarse_now,
    coarse_prev,
    fine_rho,
    fine_mu,
    fine_lam,
    fine_metric,
    coarse_rho,
    coarse_mu,
    coarse_lam,
    coarse_metric,
    couple_index,
    couple_weight,
    fine_out,
    coarse_out,
    f1,
    f2,
    c1,
    c2,
    f_old,
    c_old,
    f_par,
    c_par,
    index_in,
    weight_in,
    f_lift,
    f_bend,
    c_lift,
    c_bend,
    t2,
    mix,
    table,
    f_base,
    c_base,
    f_last,
    c_last,
    load_sem,
    out_sem,
    send_sem,
    recv_sem,
):
    nxf, nyf, layers = fine_rho.shape
    nxc, nyc, _ = coarse_rho.shape
    span = OFF + nyc
    gx, gy = lax.axis_index("gx"), lax.axis_index("gy")

    def inner(nx, ny):
        return pl.ds(2, nx), pl.ds(OFF, ny)

    def exists(dx, dy):
        ok = None
        for step, position, size in ((dx, gx, size_x), (dy, gy, size_y)):
            if step:
                here = position >= 1 if step < 0 else position <= size - 2
                ok = here if ok is None else jnp.logical_and(ok, here)
        return ok

    barrier = pltpu.get_barrier_semaphore()
    for dx, dy in DIRS:

        @pl.when(exists(dx, dy))
        def _():
            pl.semaphore_signal(
                barrier, inc=1, device_id=(gx + dx, gy + dy), device_id_type=MESH
            )

    fx, fy = inner(nxf, nyf)
    cx, cy = inner(nxc, nyc)
    pairs = [
        (coarse_now, c1.at[0:3, cx, cy]),
        (coarse_metric, c1.at[3, cx, cy]),
        (fine_now, f1.at[0:3, fx, fy]),
        (fine_metric, f1.at[3, fx, fy]),
        (coarse_rho, c_par.at[0]),
        (coarse_mu, c_par.at[1]),
        (coarse_lam, c_par.at[2]),
        (coarse_prev, c_old),
        (fine_rho, f_par.at[0]),
        (fine_mu, f_par.at[1]),
        (fine_lam, f_par.at[2]),
        (fine_prev, f_old),
        (couple_index, index_in),
        (couple_weight, weight_in),
    ]
    loads = [
        pltpu.make_async_copy(source, target, load_sem.at[n])
        for n, (source, target) in enumerate(pairs)
    ]
    for load in loads:
        load.start()

    half = vertical_table12(layers)
    table[...] = jnp.concatenate([half, half], axis=0)

    def source_range(step, start, length):
        return {-1: pl.ds(start, 2), 1: pl.ds(start + length - 2, 2), 0: pl.ds(start, length)}[step]

    def target_range(step, start, length, wrap=0):
        after = start + length - wrap
        return {-1: pl.ds(after, 2), 1: pl.ds(start - 2, 2), 0: pl.ds(start, length)}[step]

    class Exchange:
        def __init__(self, base, buffer, nx, ny, sides, corners, wrap=0):
            self.copies = []
            self.targets = []
            for n, (dx, dy) in enumerate(DIRS):
                parts = sides if n < 4 else corners
                xs, ys = source_range(dx, 2, nx), source_range(dy, OFF, ny)
                xt, yt = target_range(dx, 2, nx), target_range(dy, OFF, ny, wrap)
                if parts is None:
                    src, dst = buffer.at[xs, ys], buffer.at[xt, yt]
                    self.targets.append((buffer, (xt, yt), (xt.size, yt.size, layers)))
                else:
                    ps = pl.ds(0, parts)
                    src, dst = buffer.at[ps, xs, ys], buffer.at[ps, xt, yt]
                    self.targets.append((buffer, (ps, xt, yt), (parts, xt.size, yt.size, layers)))
                copy = pltpu.make_async_remote_copy(
                    src_ref=src,
                    dst_ref=dst,
                    send_sem=send_sem.at[base + n],
                    recv_sem=recv_sem.at[base + n],
                    device_id=(gx + dx, gy + dy),
                    device_id_type=MESH,
                )
                self.copies.append(copy)

        def start(self):
            for (dx, dy), copy in zip(DIRS, self.copies):
                pl.when(exists(dx, dy))(copy.start)

        def arrive(self):
            for (dx, dy), copy in zip(DIRS, self.copies):
                pl.when(exists(-dx, -dy))(copy.wait_recv)

        def finish(self):
            for (dx, dy), copy in zip(DIRS, self.copies):
                pl.when(exists(dx, dy))(copy.wait_send)

    coarse_a = Exchange(0, c1, nxc, nyc, 4, 2)
    fine_a = Exchange(8, f1, nxf, nyf, 4, 2)
    coarse_b = Exchange(16, c2, nxc, nyc, 3, 3)
    fine_b = Exchange(24, f2, nxf, nyf, 3, 2)
    top_c = Exchange(32, t2, nxc, nyc, None, None, wrap=span)
    exchanges = (coarse_a, fine_a, coarse_b, fine_b, top_c)

    for load in loads[0:4]:
        load.wait()
    sides_x = 1 + (gx >= 1).astype(jnp.int32) + (gx <= size_x - 2).astype(jnp.int32)
    sides_y = 1 + (gy >= 1).astype(jnp.int32) + (gy <= size_y - 2).astype(jnp.int32)
    pl.semaphore_wait(barrier, sides_x * sides_y - 1)
    coarse_a.start()
    fine_a.start()

    for n, (dx, dy) in enumerate(DIRS):

        @pl.when(jnp.logical_not(exists(-dx, -dy)))
        def _():
            for exchange in exchanges:
                buffer, where, shape = exchange.targets[n]
                buffer[where] = jnp.zeros(shape, f32)

    cells = (nxc + 4) * span

    def build_mix():
        width = nyc + 4
        reciprocal = (2048 + width - 1) // width
        index = index_in[...].reshape(nxf * nyf, -1)
        weight = weight_in[...].reshape(nxf * nyf, -1)
        row = jnp.right_shift(index * reciprocal, 11)
        column = index - row * width + (OFF - 2)
        column = jnp.where(column >= span, column - span, column)
        place = row * span + column
        cell = lax.broadcasted_iota(jnp.int32, (nxf * nyf, cells), 1)
        total = jnp.zeros((nxf * nyf, cells), f32)
        for j in range(index.shape[1]):
            total += jnp.where(cell == place[:, j : j + 1], weight[:, j : j + 1], 0.0)
        mix_high, mix_low = halves(total)
        mix[0] = mix_high
        mix[1] = mix_low

    lane = lax.broadcasted_iota(jnp.int32, (1, 1, layers), 2)

    def tops(parts):
        out = None
        for c, values in enumerate(parts):
            only = jnp.where(lane == layers - 1, values, 0.0)
            moved = pltpu.roll(only.reshape(-1, layers), c + 1, 1).reshape(values.shape)
            out = moved if out is None else out + moved
        return out

    def interface(top, parts):
        high, low = halves(top.reshape(cells, layers))
        found = dot(mix[0], high) + (dot(mix[1], high) + dot(mix[0], low))
        result = []
        for c, values in enumerate(parts):
            moved = found if c == 0 else pltpu.roll(found, layers - c, 1)
            result.append(jnp.where(lane == 0, moved.reshape(values.shape), values))
        return result

    f_in = (slice(2, 2 + nxf), slice(OFF, OFF + nyf))
    c_in = (slice(2, 2 + nxc), slice(OFF, OFF + nyc))

    def parameters(par):
        scale = (time_step * time_step) / par[0]
        shear = par[1]
        par[0] = shear * scale
        par[1] = (par[2] + shear) * scale

    def fine_before(u, earlier):
        before_halo(u, f1.at[3], f_lift, f_base, earlier, f_par[0], table[...], nxf, nyf)

    def coarse_before(u, earlier):
        before_halo(u, c1.at[3], c_lift, c_base, earlier, c_par[0], table[...], nxc, nyc)

    def fine_after(u, put):
        after_halo(
            u, f1.at[3], f_lift, f_bend, f_base, f_par[0], f_par[1], table[...], nxf, nyf, 1.0, put
        )

    def coarse_after(u, put):
        after_halo(
            u, c1.at[3], c_lift, c_bend, c_base, c_par[0], c_par[1], table[...], nxc, nyc, 2.0, put
        )

    def put_in(buffer, where):
        def put(c, values):
            buffer[c, where[0], where[1]] = values

        return put

    def put_out(buffer):
        def put(c, values):
            buffer[c] = values

        return put

    for load in loads[4:8]:
        load.wait()
    parameters(c_par)
    coarse_before(c1, lambda c: c_old[c])
    coarse_a.arrive()
    coarse_after(c1, put_in(c2, c_in))
    coarse_b.start()
    for load in loads[8:12]:
        load.wait()
    parameters(f_par)
    fine_before(f1, lambda c: f_old[c])
    for load in loads[12:]:
        load.wait()
    build_mix()
    fine_a.arrive()
    fine_after(f1, put_in(f2, f_in))
    coarse_b.arrive()
    sub = lax.broadcasted_iota(jnp.int32, (1, OFF, 1), 1)
    rims = []
    for c in range(3):
        after, before = c2[c, :, OFF + nyc : 2 * OFF + nyc], c2[c, :, 0:OFF]
        rims.append(jnp.where(sub < 2, after, jnp.where(sub >= OFF - 2, before, 0.0)))
    top = jnp.concatenate([tops(rims), tops([c2[c, :, c_in[1]] for c in range(3)])], axis=1)
    for c, values in enumerate(interface(top, [f2[c, f_in[0], f_in[1]] for c in range(3)])):
        f2[c, f_in[0], f_in[1]] = values
    fine_b.start()

    coarse_before(c2, lambda c: c1[c, c_in[0], c_in[1]])
    coarse_after(c2, put_out(c_last))
    t2[c_in[0], c_in[1]] = tops([c_last[c] for c in range(3)])
    top_c.start()
    store_coarse = pltpu.make_async_copy(c_last, coarse_out, out_sem.at[0])
    store_coarse.start()
    fine_before(f2, lambda c: f1[c, f_in[0], f_in[1]])
    fine_b.arrive()
    fine_after(f2, put_out(f_last))
    top_c.arrive()
    rim = jnp.where(jnp.logical_or(sub < 2, sub >= OFF - 2), t2[:, 0:OFF], 0.0)
    top = jnp.concatenate([rim, t2[:, OFF:span]], axis=1)
    for c, values in enumerate(interface(top, [f_last[c] for c in range(3)])):
        f_last[c] = values
    store_fine = pltpu.make_async_copy(f_last, fine_out, out_sem.at[1])
    store_fine.start()
    for exchange in exchanges:
        exchange.finish()
    store_coarse.wait()
    store_fine.wait()


def finish(fine_in, coarse_in, fine_out, coarse_out, sem):
    copies = [
        pltpu.make_async_copy(fine_in, fine_out, sem.at[0]),
        pltpu.make_async_copy(coarse_in, coarse_out, sem.at[1]),
    ]
    for copy in copies:
        copy.start()
    for copy in copies:
        copy.wait()


def solution(mesh):
    size_x, size_y = mesh.shape["gx"], mesh.shape["gy"]

    def on_device(*args):
        fine, coarse = args[0], args[2]
        _, nxf, nyf, layers = fine.shape
        _, nxc, nyc, _ = coarse.shape
        index = args[12]

        def wide(parts, nx, ny):
            return pltpu.VMEM((parts, nx + 4, ny + 2 * OFF, layers), f32)

        span = OFF + nyc
        scratch = [
            wide(4, nxf, nyf),
            wide(3, nxf, nyf),
            wide(4, nxc, nyc),
            wide(3, nxc, nyc),
            pltpu.VMEM(fine.shape, f32),
            pltpu.VMEM(coarse.shape, f32),
            pltpu.VMEM(fine.shape, f32),
            pltpu.VMEM(coarse.shape, f32),
            pltpu.VMEM(index.shape, jnp.int32),
            pltpu.VMEM(index.shape, f32),
            pltpu.VMEM((nxf + 4, nyf + 2 * OFF, layers), f32),
            pltpu.VMEM((nxf, nyf + 2 * OFF, layers), f32),
            pltpu.VMEM((nxc + 4, nyc + 2 * OFF, layers), f32),
            pltpu.VMEM((nxc, nyc + 2 * OFF, layers), f32),
            pltpu.VMEM((nxc + 4, span, layers), f32),
            pltpu.VMEM((2, nxf * nyf, (nxc + 4) * span), bf16),
            pltpu.VMEM((2 * layers, layers), bf16),
            pltpu.VMEM(fine.shape, f32),
            pltpu.VMEM(coarse.shape, f32),
            pltpu.VMEM(fine.shape, f32),
            pltpu.VMEM(coarse.shape, f32),
            pltpu.SemaphoreType.DMA((14,)),
            pltpu.SemaphoreType.DMA((2,)),
            pltpu.SemaphoreType.DMA((40,)),
            pltpu.SemaphoreType.DMA((40,)),
        ]
        shapes = (
            jax.ShapeDtypeStruct(fine.shape, f32),
            jax.ShapeDtypeStruct(coarse.shape, f32),
        )
        hbm = pl.BlockSpec(memory_space=pltpu.HBM)
        results = pl.pallas_call(
            functools.partial(kernel, size_x, size_y),
            out_shape=shapes,
            in_specs=[hbm] * 14,
            out_specs=(hbm, hbm),
            scratch_shapes=scratch,
            compiler_params=pltpu.CompilerParams(
                collective_id=0, has_side_effects=True, vmem_limit_bytes=56 * 1024 * 1024
            ),
        )(*args)
        return pl.pallas_call(
            finish,
            out_shape=shapes,
            in_specs=[hbm, hbm],
            out_specs=(hbm, hbm),
            scratch_shapes=[pltpu.SemaphoreType.DMA((2,))],
            compiler_params=pltpu.CompilerParams(vmem_limit_bytes=56 * 1024 * 1024),
        )(*results)

    field, flat = P(None, "gx", "gy", None), P("gx", "gy", None)
    return jax.shard_map(
        on_device,
        mesh=mesh,
        in_specs=(field,) * 4 + (flat,) * 10,
        out_specs=(field, field),
        check_vma=False,
    )
```

```python
import functools

import jax
import jax.numpy as jnp
from jax import lax
from jax.experimental import pallas as pl
from jax.experimental.pallas import tpu as pltpu
from jax.sharding import PartitionSpec as P

MESH = pl.DeviceIdType.MESH
f32 = jnp.float32
bf16 = jnp.bfloat16
time_step = 0.25
OFF = 8
SIDES = ((-1, 0), (1, 0), (0, -1), (0, 1))
CORNERS = ((-1, -1), (-1, 1), (1, -1), (1, 1))
DIRS = SIDES + CORNERS


def vertical_table12(layers):
    level_in = lax.broadcasted_iota(jnp.int32, (layers, layers), 0)
    level_out = lax.broadcasted_iota(jnp.int32, (layers, layers), 1)
    apart = level_in - level_out
    table = jnp.where(apart == -2, 1.0, 0.0)
    table = jnp.where(apart == -1, -8.0, table)
    table = jnp.where(apart == 1, 8.0, table)
    table = jnp.where(apart == 2, -1.0, table)
    last = layers - 1
    edges = {
        0: ((0, -18.0), (1, 24.0), (2, -6.0)),
        1: ((0, -6.0), (2, 6.0)),
        last - 1: ((last - 2, -6.0), (last, 6.0)),
        last: ((last - 2, 6.0), (last - 1, -24.0), (last, 18.0)),
    }
    for row, taps in edges.items():
        column = jnp.zeros_like(table)
        for level, value in taps:
            column = jnp.where(level_in == level, value, column)
        table = jnp.where(level_out == row, column, table)
    return table.astype(bf16)


def halves(values):
    high = values.astype(bf16)
    low = (values - high.astype(f32)).astype(bf16)
    return high, low


def dot(left, right):
    return jnp.dot(left, right, preferred_element_type=f32)


def vertical12(values, table2):
    shape = values.shape
    high, low = halves(values.reshape(-1, shape[-1]))
    return dot(jnp.concatenate([high, low], axis=1), table2).reshape(shape)


def before_halo(u, metric, lift, base, earlier, shear, table2, nx, ny):
    inner_x, inner_y = slice(2, 2 + nx), slice(OFF, OFF + ny)
    metric_in = metric[inner_x, inner_y] * (1.0 / 12.0)
    present = u[0:3, inner_x, inner_y]
    slopes = metric_in * vertical12(present, table2)
    lift[inner_x, inner_y] = slopes[2]
    bent = metric_in * vertical12(slopes, table2)
    for c in range(3):
        base[c] = 2.0 * present[c] - earlier(c) + shear * bent[c]


def after_halo(u, metric, lift, bend, base, shear, both, table2, nx, ny, spacing, put):
    inner_x, inner_y = slice(2, 2 + nx), slice(OFF, OFF + ny)
    t1 = 1.0 / (12.0 * spacing)
    t2 = 1.0 / (12.0 * spacing * spacing)

    def first(m2, m1, p1, p2):
        return t1 * ((m2 - p2) + 8.0 * (p1 - m1))

    def second(m2, m1, mid, p1, p2):
        return t2 * (16.0 * (m1 + p1) - (m2 + p2) - 30.0 * mid)

    def along_y(read):
        return [read(slice(OFF + s, OFF + s + ny)) for s in (-2, -1, 0, 1, 2)]

    def along_x(values):
        return [values[2 + s : 2 + s + nx] for s in (-2, -1, 0, 1, 2)]

    layers = u.shape[-1]
    rims = (
        (slice(0, 2), inner_y),
        (slice(2 + nx, 4 + nx), inner_y),
        (inner_x, slice(0, OFF)),
        (inner_x, slice(OFF + ny, 2 * OFF + ny)),
    )
    rows = [u[2, xs, ys].reshape(-1, layers) for xs, ys in rims]
    found = vertical12(jnp.concatenate(rows, axis=0), table2)
    start = 0
    for (xs, ys), part in zip(rims, rows):
        scale = metric[xs, ys] * (1.0 / 12.0)
        lift[xs, ys] = scale * found[start : start + part.shape[0]].reshape(scale.shape)
        start += part.shape[0]

    m2, m1, mid, p1, p2 = along_x(u[0])
    bend[...] = first(m2, m1, p1, p2) + lift[inner_x]
    curve_x0 = second(*[v[:, inner_y] for v in (m2, m1, mid, p1, p2)])
    slope_x0 = bend[:, inner_y]

    m2, m1, mid, p1, p2 = along_y(lambda ys: u[1, :, ys])
    slant = first(m2, m1, p1, p2) + lift[:, inner_y]
    spread = slant[inner_x] + slope_x0 - lift[inner_x, inner_y]
    bent = (metric[inner_x, inner_y] * (1.0 / 12.0)) * vertical12(spread, table2)
    curve_y1 = second(*[v[inner_x] for v in (m2, m1, mid, p1, p2)])
    curve_x1 = second(*along_x(mid))
    m2, m1, _, p1, p2 = along_x(slant)
    graddiv_0 = curve_x0 + first(m2, m1, p1, p2)
    curve_y0 = second(*along_y(lambda ys: u[0, inner_x, ys]))
    put(0, base[0] + shear * (curve_x0 + curve_y0) + both * graddiv_0)

    m2, m1, mid, p1, p2 = along_y(lambda ys: bend[:, ys])
    graddiv_1 = curve_y1 + first(m2, m1, p1, p2)
    put(1, base[1] + shear * (curve_x1 + curve_y1) + both * graddiv_1)

    curve_2 = second(*along_x(u[2, :, inner_y])) + second(*along_y(lambda ys: u[2, inner_x, ys]))
    put(2, base[2] + shear * curve_2 + both * bent)


def kernel(
    size_x,
    size_y,
    fine_now,
    fine_prev,
    coarse_now,
    coarse_prev,
    fine_rho,
    fine_mu,
    fine_lam,
    fine_metric,
    coarse_rho,
    coarse_mu,
    coarse_lam,
    coarse_metric,
    couple_index,
    couple_weight,
    fine_out,
    coarse_out,
    f1,
    f2,
    c1,
    c2,
    f_old,
    c_old,
    f_par,
    c_par,
    index_in,
    weight_in,
    f_lift,
    f_bend,
    c_lift,
    c_bend,
    t2,
    mix,
    table,
    f_base,
    c_base,
    load_sem,
    send_sem,
    recv_sem,
):
    nxf, nyf, layers = fine_rho.shape
    nxc, nyc, _ = coarse_rho.shape
    span = OFF + nyc
    gx, gy = lax.axis_index("gx"), lax.axis_index("gy")

    def inner(nx, ny):
        return pl.ds(2, nx), pl.ds(OFF, ny)

    def exists(dx, dy):
        ok = None
        for step, position, size in ((dx, gx, size_x), (dy, gy, size_y)):
            if step:
                here = position >= 1 if step < 0 else position <= size - 2
                ok = here if ok is None else jnp.logical_and(ok, here)
        return ok

    barrier = pltpu.get_barrier_semaphore()
    for dx, dy in DIRS:

        @pl.when(exists(dx, dy))
        def _():
            pl.semaphore_signal(
                barrier, inc=1, device_id=(gx + dx, gy + dy), device_id_type=MESH
            )

    fx, fy = inner(nxf, nyf)
    cx, cy = inner(nxc, nyc)
    pairs = [
        (coarse_now, c1.at[0:3, cx, cy]),
        (coarse_metric, c1.at[3, cx, cy]),
        (fine_now, f1.at[0:3, fx, fy]),
        (fine_metric, f1.at[3, fx, fy]),
        (coarse_rho, c_par.at[0]),
        (coarse_mu, c_par.at[1]),
        (coarse_lam, c_par.at[2]),
        (coarse_prev, c_old),
        (fine_rho, f_par.at[0]),
        (fine_mu, f_par.at[1]),
        (fine_lam, f_par.at[2]),
        (fine_prev, f_old),
        (couple_index, index_in),
        (couple_weight, weight_in),
    ]
    loads = [
        pltpu.make_async_copy(source, target, load_sem.at[n])
        for n, (source, target) in enumerate(pairs)
    ]
    for load in loads:
        load.start()

    half = vertical_table12(layers)
    table[...] = jnp.concatenate([half, half], axis=0)

    def source_range(step, start, length):
        return {-1: pl.ds(start, 2), 1: pl.ds(start + length - 2, 2), 0: pl.ds(start, length)}[step]

    def target_range(step, start, length, wrap=0):
        after = start + length - wrap
        return {-1: pl.ds(after, 2), 1: pl.ds(start - 2, 2), 0: pl.ds(start, length)}[step]

    class Exchange:
        def __init__(self, base, buffer, nx, ny, sides, corners, wrap=0):
            self.copies = []
            self.targets = []
            for n, (dx, dy) in enumerate(DIRS):
                parts = sides if n < 4 else corners
                xs, ys = source_range(dx, 2, nx), source_range(dy, OFF, ny)
                xt, yt = target_range(dx, 2, nx), target_range(dy, OFF, ny, wrap)
                if parts is None:
                    src, dst = buffer.at[xs, ys], buffer.at[xt, yt]
                    self.targets.append((buffer, (xt, yt), (xt.size, yt.size, layers)))
                else:
                    ps = pl.ds(0, parts)
                    src, dst = buffer.at[ps, xs, ys], buffer.at[ps, xt, yt]
                    self.targets.append((buffer, (ps, xt, yt), (parts, xt.size, yt.size, layers)))
                copy = pltpu.make_async_remote_copy(
                    src_ref=src,
                    dst_ref=dst,
                    send_sem=send_sem.at[base + n],
                    recv_sem=recv_sem.at[base + n],
                    device_id=(gx + dx, gy + dy),
                    device_id_type=MESH,
                )
                self.copies.append(copy)

        def start(self):
            for n in (4, 5, 6, 7, 0, 1, 2, 3):
                pl.when(exists(*DIRS[n]))(self.copies[n].start)

        def arrive(self):
            for (dx, dy), copy in zip(DIRS, self.copies):
                pl.when(exists(-dx, -dy))(copy.wait_recv)

        def finish(self):
            for (dx, dy), copy in zip(DIRS, self.copies):
                pl.when(exists(dx, dy))(copy.wait_send)

    coarse_a = Exchange(0, c1, nxc, nyc, 4, 2)
    fine_a = Exchange(8, f1, nxf, nyf, 4, 2)
    coarse_b = Exchange(16, c2, nxc, nyc, 3, 3)
    fine_b = Exchange(24, f2, nxf, nyf, 3, 2)
    top_c = Exchange(32, t2, nxc, nyc, None, None, wrap=span)
    exchanges = (coarse_a, fine_a, coarse_b, fine_b, top_c)

    for load in loads[0:4]:
        load.wait()
    sides_x = 1 + (gx >= 1).astype(jnp.int32) + (gx <= size_x - 2).astype(jnp.int32)
    sides_y = 1 + (gy >= 1).astype(jnp.int32) + (gy <= size_y - 2).astype(jnp.int32)
    pl.semaphore_wait(barrier, sides_x * sides_y - 1)
    coarse_a.start()
    fine_a.start()

    for n, (dx, dy) in enumerate(DIRS):

        @pl.when(jnp.logical_not(exists(-dx, -dy)))
        def _():
            for exchange in exchanges:
                buffer, where, shape = exchange.targets[n]
                buffer[where] = jnp.zeros(shape, f32)

    cells = (nxc + 4) * span

    def build_mix():
        width = nyc + 4
        reciprocal = (2048 + width - 1) // width
        index = index_in[...].reshape(nxf * nyf, -1)
        weight = weight_in[...].reshape(nxf * nyf, -1)
        row = jnp.right_shift(index * reciprocal, 11)
        column = index - row * width + (OFF - 2)
        column = jnp.where(column >= span, column - span, column)
        place = row * span + column
        cell = lax.broadcasted_iota(jnp.int32, (nxf * nyf, cells), 1)
        total = jnp.zeros((nxf * nyf, cells), f32)
        for j in range(index.shape[1]):
            total += jnp.where(cell == place[:, j : j + 1], weight[:, j : j + 1], 0.0)
        mix_high, mix_low = halves(total)
        mix[0] = mix_high
        mix[1] = mix_low

    lane = lax.broadcasted_iota(jnp.int32, (1, 1, layers), 2)

    def tops(parts):
        out = None
        for c, values in enumerate(parts):
            only = jnp.where(lane == layers - 1, values, 0.0)
            moved = pltpu.roll(only.reshape(-1, layers), c + 1, 1).reshape(values.shape)
            out = moved if out is None else out + moved
        return out

    def interface(top, parts):
        high, low = halves(top.reshape(cells, layers))
        found = dot(mix[0], high) + (dot(mix[1], high) + dot(mix[0], low))
        result = []
        for c, values in enumerate(parts):
            moved = found if c == 0 else pltpu.roll(found, layers - c, 1)
            result.append(jnp.where(lane == 0, moved.reshape(values.shape), values))
        return result

    f_in = (slice(2, 2 + nxf), slice(OFF, OFF + nyf))
    c_in = (slice(2, 2 + nxc), slice(OFF, OFF + nyc))

    def parameters(par):
        scale = (time_step * time_step) / par[0]
        shear = par[1]
        par[0] = shear * scale
        par[1] = (par[2] + shear) * scale

    def fine_before(u, earlier):
        before_halo(u, f1.at[3], f_lift, f_base, earlier, f_par[0], table[...], nxf, nyf)

    def coarse_before(u, earlier):
        before_halo(u, c1.at[3], c_lift, c_base, earlier, c_par[0], table[...], nxc, nyc)

    def fine_after(u, put):
        after_halo(
            u, f1.at[3], f_lift, f_bend, f_base, f_par[0], f_par[1], table[...], nxf, nyf, 1.0, put
        )

    def coarse_after(u, put):
        after_halo(
            u, c1.at[3], c_lift, c_bend, c_base, c_par[0], c_par[1], table[...], nxc, nyc, 2.0, put
        )

    def put_in(buffer, where):
        def put(c, values):
            buffer[c, where[0], where[1]] = values

        return put

    def put_out(buffer):
        def put(c, values):
            buffer[c] = values

        return put

    for load in loads[4:8]:
        load.wait()
    parameters(c_par)
    coarse_before(c1, lambda c: c_old[c])
    coarse_a.arrive()
    coarse_after(c1, put_in(c2, c_in))
    coarse_b.start()
    for load in loads[8:12]:
        load.wait()
    parameters(f_par)
    fine_before(f1, lambda c: f_old[c])
    for load in loads[12:]:
        load.wait()
    build_mix()
    fine_a.arrive()
    fine_after(f1, put_in(f2, f_in))
    coarse_b.arrive()
    sub = lax.broadcasted_iota(jnp.int32, (1, OFF, 1), 1)
    rims = []
    for c in range(3):
        after, before = c2[c, :, OFF + nyc : 2 * OFF + nyc], c2[c, :, 0:OFF]
        rims.append(jnp.where(sub < 2, after, jnp.where(sub >= OFF - 2, before, 0.0)))
    top = jnp.concatenate([tops(rims), tops([c2[c, :, c_in[1]] for c in range(3)])], axis=1)
    for c, values in enumerate(interface(top, [f2[c, f_in[0], f_in[1]] for c in range(3)])):
        f2[c, f_in[0], f_in[1]] = values
    fine_b.start()

    coarse_before(c2, lambda c: c1[c, c_in[0], c_in[1]])
    coarse_after(c2, put_out(coarse_out))
    t2[c_in[0], c_in[1]] = tops([coarse_out[c] for c in range(3)])
    top_c.start()
    fine_before(f2, lambda c: f1[c, f_in[0], f_in[1]])
    fine_b.arrive()
    fine_after(f2, put_out(fine_out))
    top_c.arrive()
    rim = jnp.where(jnp.logical_or(sub < 2, sub >= OFF - 2), t2[:, 0:OFF], 0.0)
    top = jnp.concatenate([rim, t2[:, OFF:span]], axis=1)
    for c, values in enumerate(interface(top, [fine_out[c] for c in range(3)])):
        fine_out[c] = values
    for exchange in exchanges:
        exchange.finish()


def finish(fine_in, coarse_in, fine_out, coarse_out, sem):
    copies = [
        pltpu.make_async_copy(fine_in, fine_out, sem.at[0]),
        pltpu.make_async_copy(coarse_in, coarse_out, sem.at[1]),
    ]
    for copy in copies:
        copy.start()
    for copy in copies:
        copy.wait()


def solution(mesh):
    size_x, size_y = mesh.shape["gx"], mesh.shape["gy"]

    def on_device(*args):
        fine, coarse = args[0], args[2]
        _, nxf, nyf, layers = fine.shape
        _, nxc, nyc, _ = coarse.shape
        index = args[12]

        def wide(parts, nx, ny):
            return pltpu.VMEM((parts, nx + 4, ny + 2 * OFF, layers), f32)

        span = OFF + nyc
        scratch = [
            wide(4, nxf, nyf),
            wide(3, nxf, nyf),
            wide(4, nxc, nyc),
            wide(3, nxc, nyc),
            pltpu.VMEM(fine.shape, f32),
            pltpu.VMEM(coarse.shape, f32),
            pltpu.VMEM(fine.shape, f32),
            pltpu.VMEM(coarse.shape, f32),
            pltpu.VMEM(index.shape, jnp.int32),
            pltpu.VMEM(index.shape, f32),
            pltpu.VMEM((nxf + 4, nyf + 2 * OFF, layers), f32),
            pltpu.VMEM((nxf, nyf + 2 * OFF, layers), f32),
            pltpu.VMEM((nxc + 4, nyc + 2 * OFF, layers), f32),
            pltpu.VMEM((nxc, nyc + 2 * OFF, layers), f32),
            pltpu.VMEM((nxc + 4, span, layers), f32),
            pltpu.VMEM((2, nxf * nyf, (nxc + 4) * span), bf16),
            pltpu.VMEM((2 * layers, layers), bf16),
            pltpu.VMEM(fine.shape, f32),
            pltpu.VMEM(coarse.shape, f32),
            pltpu.SemaphoreType.DMA((14,)),
            pltpu.SemaphoreType.DMA((40,)),
            pltpu.SemaphoreType.DMA((40,)),
        ]
        shapes = (
            jax.ShapeDtypeStruct(fine.shape, f32),
            jax.ShapeDtypeStruct(coarse.shape, f32),
        )
        hbm, vmem = pl.BlockSpec(memory_space=pltpu.HBM), pl.BlockSpec(memory_space=pltpu.VMEM)
        args = [pltpu.with_memory_space_constraint(arg, pltpu.HBM) for arg in args]
        results = pl.pallas_call(
            functools.partial(kernel, size_x, size_y),
            out_shape=(pltpu.VMEM(fine.shape, f32), pltpu.VMEM(coarse.shape, f32)),
            in_specs=[hbm] * 14,
            out_specs=(vmem, vmem),
            scratch_shapes=scratch,
            compiler_params=pltpu.CompilerParams(
                collective_id=0, has_side_effects=True, vmem_limit_bytes=32 * 1024 * 1024
            ),
        )(*args)
        return pl.pallas_call(
            finish,
            out_shape=shapes,
            in_specs=[vmem, vmem],
            out_specs=(hbm, hbm),
            scratch_shapes=[pltpu.SemaphoreType.DMA((2,))],
            compiler_params=pltpu.CompilerParams(vmem_limit_bytes=16 * 1024 * 1024),
        )(*results)

    field, flat = P(None, "gx", "gy", None), P("gx", "gy", None)
    return jax.shard_map(
        on_device,
        mesh=mesh,
        in_specs=(field,) * 4 + (flat,) * 10,
        out_specs=(field, field),
        check_vma=False,
    )
```

```python
import functools

import jax
import jax.numpy as jnp
from jax import lax
from jax.experimental import pallas as pl
from jax.experimental.pallas import tpu as pltpu
from jax.sharding import PartitionSpec as P

MESH = pl.DeviceIdType.MESH
f32 = jnp.float32
bf16 = jnp.bfloat16
time_step = 0.25
OFF = 8
SIDES = ((-1, 0), (1, 0), (0, -1), (0, 1))
CORNERS = ((-1, -1), (-1, 1), (1, -1), (1, 1))
DIRS = SIDES + CORNERS


def vertical_table12(layers):
    level_in = lax.broadcasted_iota(jnp.int32, (layers, layers), 0)
    level_out = lax.broadcasted_iota(jnp.int32, (layers, layers), 1)
    apart = level_in - level_out
    table = jnp.where(apart == -2, 1.0, 0.0)
    table = jnp.where(apart == -1, -8.0, table)
    table = jnp.where(apart == 1, 8.0, table)
    table = jnp.where(apart == 2, -1.0, table)
    last = layers - 1
    edges = {
        0: ((0, -18.0), (1, 24.0), (2, -6.0)),
        1: ((0, -6.0), (2, 6.0)),
        last - 1: ((last - 2, -6.0), (last, 6.0)),
        last: ((last - 2, 6.0), (last - 1, -24.0), (last, 18.0)),
    }
    for row, taps in edges.items():
        column = jnp.zeros_like(table)
        for level, value in taps:
            column = jnp.where(level_in == level, value, column)
        table = jnp.where(level_out == row, column, table)
    return table.astype(bf16)


def halves(values):
    high = values.astype(bf16)
    low = (values - high.astype(f32)).astype(bf16)
    return high, low


def dot(left, right):
    return jnp.dot(left, right, preferred_element_type=f32)


def vertical12(values, table2):
    shape = values.shape
    high, low = halves(values.reshape(-1, shape[-1]))
    return dot(jnp.concatenate([high, low], axis=1), table2).reshape(shape)


def before_halo(u, metric, lift, base, earlier, shear, table2, nx, ny):
    inner_x, inner_y = slice(2, 2 + nx), slice(OFF, OFF + ny)
    metric_in = metric[inner_x, inner_y] * (1.0 / 12.0)
    present = u[0:3, inner_x, inner_y]
    slopes = metric_in * vertical12(present, table2)
    lift[inner_x, inner_y] = slopes[2]
    bent = metric_in * vertical12(slopes, table2)
    for c in range(3):
        base[c] = 2.0 * present[c] - earlier(c) + shear * bent[c]


def after_halo(u, metric, lift, bend, base, shear, both, table2, nx, ny, spacing, put):
    inner_x, inner_y = slice(2, 2 + nx), slice(OFF, OFF + ny)
    t1 = 1.0 / (12.0 * spacing)
    t2 = 1.0 / (12.0 * spacing * spacing)

    def first(m2, m1, p1, p2):
        return t1 * ((m2 - p2) + 8.0 * (p1 - m1))

    def second(m2, m1, mid, p1, p2):
        return t2 * (16.0 * (m1 + p1) - (m2 + p2) - 30.0 * mid)

    def along_y(read):
        return [read(slice(OFF + s, OFF + s + ny)) for s in (-2, -1, 0, 1, 2)]

    def along_x(values):
        return [values[2 + s : 2 + s + nx] for s in (-2, -1, 0, 1, 2)]

    layers = u.shape[-1]
    rims = (
        (slice(0, 2), inner_y),
        (slice(2 + nx, 4 + nx), inner_y),
        (inner_x, slice(0, OFF)),
        (inner_x, slice(OFF + ny, 2 * OFF + ny)),
    )
    rows = [u[2, xs, ys].reshape(-1, layers) for xs, ys in rims]
    found = vertical12(jnp.concatenate(rows, axis=0), table2)
    start = 0
    for (xs, ys), part in zip(rims, rows):
        scale = metric[xs, ys] * (1.0 / 12.0)
        lift[xs, ys] = scale * found[start : start + part.shape[0]].reshape(scale.shape)
        start += part.shape[0]

    m2, m1, mid, p1, p2 = along_x(u[0])
    bend[...] = first(m2, m1, p1, p2) + lift[inner_x]
    curve_x0 = second(*[v[:, inner_y] for v in (m2, m1, mid, p1, p2)])
    slope_x0 = bend[:, inner_y]

    m2, m1, mid, p1, p2 = along_y(lambda ys: u[1, :, ys])
    slant = first(m2, m1, p1, p2) + lift[:, inner_y]
    spread = slant[inner_x] + slope_x0 - lift[inner_x, inner_y]
    bent = (metric[inner_x, inner_y] * (1.0 / 12.0)) * vertical12(spread, table2)
    curve_y1 = second(*[v[inner_x] for v in (m2, m1, mid, p1, p2)])
    curve_x1 = second(*along_x(mid))
    m2, m1, _, p1, p2 = along_x(slant)
    graddiv_0 = curve_x0 + first(m2, m1, p1, p2)
    curve_y0 = second(*along_y(lambda ys: u[0, inner_x, ys]))
    put(0, base[0] + shear * (curve_x0 + curve_y0) + both * graddiv_0)

    m2, m1, mid, p1, p2 = along_y(lambda ys: bend[:, ys])
    graddiv_1 = curve_y1 + first(m2, m1, p1, p2)
    put(1, base[1] + shear * (curve_x1 + curve_y1) + both * graddiv_1)

    curve_2 = second(*along_x(u[2, :, inner_y])) + second(*along_y(lambda ys: u[2, inner_x, ys]))
    put(2, base[2] + shear * curve_2 + both * bent)


def kernel(
    size_x,
    size_y,
    fine_now,
    fine_prev,
    coarse_now,
    coarse_prev,
    fine_rho,
    fine_mu,
    fine_lam,
    fine_metric,
    coarse_rho,
    coarse_mu,
    coarse_lam,
    coarse_metric,
    couple_index,
    couple_weight,
    fine_out,
    coarse_out,
    f_all,
    c_all,
    f_par,
    c_par,
    index_in,
    weight_in,
    f_lift,
    f_bend,
    c_lift,
    c_bend,
    mix,
    table,
    f_base,
    c_base,
    load_sem,
    send_sem,
    recv_sem,
):
    nxf, nyf, layers = fine_rho.shape
    nxc, nyc, _ = coarse_rho.shape
    span = OFF + nyc
    gx, gy = lax.axis_index("gx"), lax.axis_index("gy")

    def inner(nx, ny):
        return pl.ds(2, nx), pl.ds(OFF, ny)

    def exists(dx, dy):
        ok = None
        for step, position, size in ((dx, gx, size_x), (dy, gy, size_y)):
            if step:
                here = position >= 1 if step < 0 else position <= size - 2
                ok = here if ok is None else jnp.logical_and(ok, here)
        return ok

    barrier = pltpu.get_barrier_semaphore()
    for dx, dy in DIRS:

        @pl.when(exists(dx, dy))
        def _():
            pl.semaphore_signal(
                barrier, inc=1, device_id=(gx + dx, gy + dy), device_id_type=MESH
            )

    fx, fy = inner(nxf, nyf)
    cx, cy = inner(nxc, nyc)
    pairs = [
        (coarse_now, c_all.at[1, 0:3, cx, cy]),
        (coarse_metric, c_all.at[1, 3, cx, cy]),
        (fine_now, f_all.at[1, 0:3, fx, fy]),
        (fine_metric, f_all.at[1, 3, fx, fy]),
        (coarse_rho, c_par.at[0]),
        (coarse_mu, c_par.at[1]),
        (coarse_lam, c_par.at[2]),
        (coarse_prev, c_all.at[0, 0:3, cx, cy]),
        (fine_rho, f_par.at[0]),
        (fine_mu, f_par.at[1]),
        (fine_lam, f_par.at[2]),
        (fine_prev, f_all.at[0, 0:3, fx, fy]),
        (couple_index, index_in),
        (couple_weight, weight_in),
    ]
    loads = [
        pltpu.make_async_copy(source, target, load_sem.at[n])
        for n, (source, target) in enumerate(pairs)
    ]
    for load in loads:
        load.start()

    half = vertical_table12(layers)
    table[...] = jnp.concatenate([half, half], axis=0)

    def source_range(step, start, length):
        return {-1: pl.ds(start, 2), 1: pl.ds(start + length - 2, 2), 0: pl.ds(start, length)}[step]

    def target_range(step, start, length):
        return {-1: pl.ds(start + length, 2), 1: pl.ds(start - 2, 2), 0: pl.ds(start, length)}[step]

    class Exchange:
        def __init__(self, base, buffer, slot, nx, ny, sides, corners):
            self.buffer, self.slot = buffer, slot
            self.copies = []
            self.targets = []
            for n, (dx, dy) in enumerate(DIRS):
                parts = sides if n < 4 else corners
                xs, ys = source_range(dx, 2, nx), source_range(dy, OFF, ny)
                xt, yt = target_range(dx, 2, nx), target_range(dy, OFF, ny)
                ps = pl.ds(0, parts)
                self.targets.append(((slot, ps, xt, yt), (parts, xt.size, yt.size, layers)))
                copy = pltpu.make_async_remote_copy(
                    src_ref=buffer.at[slot, ps, xs, ys],
                    dst_ref=buffer.at[slot, ps, xt, yt],
                    send_sem=send_sem.at[base + n],
                    recv_sem=recv_sem.at[base + n],
                    device_id=(gx + dx, gy + dy),
                    device_id_type=MESH,
                )
                self.copies.append(copy)

        def start(self):
            for n in (4, 5, 6, 7, 0, 1, 2, 3):
                pl.when(exists(*DIRS[n]))(self.copies[n].start)

        def arrive(self):
            for (dx, dy), copy in zip(DIRS, self.copies):
                pl.when(exists(-dx, -dy))(copy.wait_recv)

        def finish(self):
            for (dx, dy), copy in zip(DIRS, self.copies):
                pl.when(exists(dx, dy))(copy.wait_send)

    def coarse_next(step):
        return Exchange(16 + 8 * step, c_all, 2 + step, nxc, nyc, 3, 3)

    coarse_a = Exchange(0, c_all, 1, nxc, nyc, 4, 2)
    fine_a = Exchange(8, f_all, 1, nxf, nyf, 4, 2)
    fine_b = Exchange(32, f_all, 2, nxf, nyf, 3, 2)
    exchanges = (coarse_a, fine_a, coarse_next(0), fine_b, coarse_next(1))

    for load in loads[0:4]:
        load.wait()
    sides_x = 1 + (gx >= 1).astype(jnp.int32) + (gx <= size_x - 2).astype(jnp.int32)
    sides_y = 1 + (gy >= 1).astype(jnp.int32) + (gy <= size_y - 2).astype(jnp.int32)
    pl.semaphore_wait(barrier, sides_x * sides_y - 1)
    coarse_a.start()
    fine_a.start()

    for n, (dx, dy) in enumerate(DIRS):

        @pl.when(jnp.logical_not(exists(-dx, -dy)))
        def _():
            for exchange in exchanges:
                where, shape = exchange.targets[n]
                exchange.buffer[where] = jnp.zeros(shape, f32)

    cells = (nxc + 4) * span

    def build_mix():
        width = nyc + 4
        reciprocal = (2048 + width - 1) // width
        index = index_in[...].reshape(nxf * nyf, -1)
        weight = weight_in[...].reshape(nxf * nyf, -1)
        row = jnp.right_shift(index * reciprocal, 11)
        column = index - row * width + (OFF - 2)
        column = jnp.where(column >= span, column - span, column)
        place = row * span + column
        cell = lax.broadcasted_iota(jnp.int32, (nxf * nyf, cells), 1)
        total = jnp.zeros((nxf * nyf, cells), f32)
        for j in range(index.shape[1]):
            total += jnp.where(cell == place[:, j : j + 1], weight[:, j : j + 1], 0.0)
        mix_high, mix_low = halves(total)
        mix[0] = mix_high
        mix[1] = mix_low

    lane = lax.broadcasted_iota(jnp.int32, (1, 1, layers), 2)

    def tops(parts):
        out = None
        for c, values in enumerate(parts):
            only = jnp.where(lane == layers - 1, values, 0.0)
            moved = pltpu.roll(only.reshape(-1, layers), c + 1, 1).reshape(values.shape)
            out = moved if out is None else out + moved
        return out

    def interface(top, parts):
        high, low = halves(top.reshape(cells, layers))
        found = dot(mix[0], high) + (dot(mix[1], high) + dot(mix[0], low))
        result = []
        for c, values in enumerate(parts):
            moved = found if c == 0 else pltpu.roll(found, layers - c, 1)
            result.append(jnp.where(lane == 0, moved.reshape(values.shape), values))
        return result

    f_in = (slice(2, 2 + nxf), slice(OFF, OFF + nyf))
    c_in = (slice(2, 2 + nxc), slice(OFF, OFF + nyc))

    def parameters(par):
        scale = (time_step * time_step) / par[0]
        shear = par[1]
        par[0] = shear * scale
        par[1] = (par[2] + shear) * scale

    f_metric, c_metric = f_all.at[1, 3], c_all.at[1, 3]
    sub = lax.broadcasted_iota(jnp.int32, (1, OFF, 1), 1)

    def put_in(buffer, slot, where):
        def put(c, values):
            buffer[slot, c, where[0], where[1]] = values

        return put

    def march(step, carry):
        u_f, u_c = f_all.at[step + 1], c_all.at[step + 1]
        coarse_b = coarse_next(step)
        before_halo(
            u_c,
            c_metric,
            c_lift,
            c_base,
            lambda c: c_all[step, c, c_in[0], c_in[1]],
            c_par[0],
            table[...],
            nxc,
            nyc,
        )
        pl.when(step == 0)(coarse_a.arrive)
        after_halo(
            u_c,
            c_metric,
            c_lift,
            c_bend,
            c_base,
            c_par[0],
            c_par[1],
            table[...],
            nxc,
            nyc,
            2.0,
            put_in(c_all, step + 2, c_in),
        )
        coarse_b.start()
        before_halo(
            u_f,
            f_metric,
            f_lift,
            f_base,
            lambda c: f_all[step, c, f_in[0], f_in[1]],
            f_par[0],
            table[...],
            nxf,
            nyf,
        )
        pl.when(step == 0)(fine_a.arrive)
        pl.when(step == 1)(fine_b.arrive)
        after_halo(
            u_f,
            f_metric,
            f_lift,
            f_bend,
            f_base,
            f_par[0],
            f_par[1],
            table[...],
            nxf,
            nyf,
            1.0,
            put_in(f_all, step + 2, f_in),
        )
        coarse_b.arrive()
        rims = []
        for c in range(3):
            after = c_all[step + 2, c, :, OFF + nyc : 2 * OFF + nyc]
            before = c_all[step + 2, c, :, 0:OFF]
            rims.append(jnp.where(sub < 2, after, jnp.where(sub >= OFF - 2, before, 0.0)))
        middle = [c_all[step + 2, c, :, c_in[1]] for c in range(3)]
        top = jnp.concatenate([tops(rims), tops(middle)], axis=1)
        parts = [f_all[step + 2, c, f_in[0], f_in[1]] for c in range(3)]
        for c, values in enumerate(interface(top, parts)):
            f_all[step + 2, c, f_in[0], f_in[1]] = values
        pl.when(step == 0)(fine_b.start)
        return carry

    for load in loads[4:]:
        load.wait()
    parameters(c_par)
    parameters(f_par)
    build_mix()
    lax.fori_loop(0, 2, march, 0)
    coarse_out[...] = c_all[3, 0:3, c_in[0], c_in[1]]
    fine_out[...] = f_all[3, 0:3, f_in[0], f_in[1]]
    for exchange in exchanges:
        exchange.finish()


def finish(fine_in, coarse_in, fine_out, coarse_out, sem):
    copies = [
        pltpu.make_async_copy(fine_in, fine_out, sem.at[0]),
        pltpu.make_async_copy(coarse_in, coarse_out, sem.at[1]),
    ]
    for copy in copies:
        copy.start()
    for copy in copies:
        copy.wait()


def solution(mesh):
    size_x, size_y = mesh.shape["gx"], mesh.shape["gy"]

    def on_device(*args):
        fine, coarse = args[0], args[2]
        _, nxf, nyf, layers = fine.shape
        _, nxc, nyc, _ = coarse.shape
        index = args[12]

        def wide(nx, ny):
            return pltpu.VMEM((4, 4, nx + 4, ny + 2 * OFF, layers), f32)

        span = OFF + nyc
        scratch = [
            wide(nxf, nyf),
            wide(nxc, nyc),
            pltpu.VMEM(fine.shape, f32),
            pltpu.VMEM(coarse.shape, f32),
            pltpu.VMEM(index.shape, jnp.int32),
            pltpu.VMEM(index.shape, f32),
            pltpu.VMEM((nxf + 4, nyf + 2 * OFF, layers), f32),
            pltpu.VMEM((nxf, nyf + 2 * OFF, layers), f32),
            pltpu.VMEM((nxc + 4, nyc + 2 * OFF, layers), f32),
            pltpu.VMEM((nxc, nyc + 2 * OFF, layers), f32),
            pltpu.VMEM((2, nxf * nyf, (nxc + 4) * span), bf16),
            pltpu.VMEM((2 * layers, layers), bf16),
            pltpu.VMEM(fine.shape, f32),
            pltpu.VMEM(coarse.shape, f32),
            pltpu.SemaphoreType.DMA((14,)),
            pltpu.SemaphoreType.DMA((40,)),
            pltpu.SemaphoreType.DMA((40,)),
        ]
        shapes = (
            jax.ShapeDtypeStruct(fine.shape, f32),
            jax.ShapeDtypeStruct(coarse.shape, f32),
        )
        hbm, vmem = pl.BlockSpec(memory_space=pltpu.HBM), pl.BlockSpec(memory_space=pltpu.VMEM)
        args = [pltpu.with_memory_space_constraint(arg, pltpu.HBM) for arg in args]
        results = pl.pallas_call(
            functools.partial(kernel, size_x, size_y),
            out_shape=(pltpu.VMEM(fine.shape, f32), pltpu.VMEM(coarse.shape, f32)),
            in_specs=[hbm] * 14,
            out_specs=(vmem, vmem),
            scratch_shapes=scratch,
            compiler_params=pltpu.CompilerParams(
                collective_id=0, has_side_effects=True, vmem_limit_bytes=32 * 1024 * 1024
            ),
        )(*args)
        return pl.pallas_call(
            finish,
            out_shape=shapes,
            in_specs=[vmem, vmem],
            out_specs=(hbm, hbm),
            scratch_shapes=[pltpu.SemaphoreType.DMA((2,))],
            compiler_params=pltpu.CompilerParams(vmem_limit_bytes=16 * 1024 * 1024),
        )(*results)

    field, flat = P(None, "gx", "gy", None), P("gx", "gy", None)
    return jax.shard_map(
        on_device,
        mesh=mesh,
        in_specs=(field,) * 4 + (flat,) * 10,
        out_specs=(field, field),
        check_vma=False,
    )
```

```python
import functools

import jax
import jax.numpy as jnp
from jax import lax
from jax.experimental import pallas as pl
from jax.experimental.pallas import tpu as pltpu
from jax.sharding import PartitionSpec as P

MESH = pl.DeviceIdType.MESH
f32 = jnp.float32
bf16 = jnp.bfloat16
time_step = 0.25
OFF = 8
SIDES = ((-1, 0), (1, 0), (0, -1), (0, 1))
CORNERS = ((-1, -1), (-1, 1), (1, -1), (1, 1))
DIRS = SIDES + CORNERS


def vertical_table12(layers):
    level_in = lax.broadcasted_iota(jnp.int32, (layers, layers), 0)
    level_out = lax.broadcasted_iota(jnp.int32, (layers, layers), 1)
    apart = level_in - level_out
    table = jnp.where(apart == -2, 1.0, 0.0)
    table = jnp.where(apart == -1, -8.0, table)
    table = jnp.where(apart == 1, 8.0, table)
    table = jnp.where(apart == 2, -1.0, table)
    last = layers - 1
    edges = {
        0: ((0, -18.0), (1, 24.0), (2, -6.0)),
        1: ((0, -6.0), (2, 6.0)),
        last - 1: ((last - 2, -6.0), (last, 6.0)),
        last: ((last - 2, 6.0), (last - 1, -24.0), (last, 18.0)),
    }
    for row, taps in edges.items():
        column = jnp.zeros_like(table)
        for level, value in taps:
            column = jnp.where(level_in == level, value, column)
        table = jnp.where(level_out == row, column, table)
    return table.astype(bf16)


def halves(values):
    high = values.astype(bf16)
    low = (values - high.astype(f32)).astype(bf16)
    return high, low


def dot(left, right):
    return jnp.dot(left, right, preferred_element_type=f32)


def vertical12(values, table2):
    shape = values.shape
    high, low = halves(values.reshape(-1, shape[-1]))
    return dot(jnp.concatenate([high, low], axis=1), table2).reshape(shape)


def before_halo(u, metric, lift, base, earlier, shear, table2, nx, ny):
    inner_x, inner_y = slice(2, 2 + nx), slice(OFF, OFF + ny)
    metric_in = metric[inner_x, inner_y] * (1.0 / 12.0)
    present = u[0:3, inner_x, inner_y]
    slopes = metric_in * vertical12(present, table2)
    lift[inner_x, inner_y] = slopes[2]
    bent = metric_in * vertical12(slopes, table2)
    for c in range(3):
        base[c] = 2.0 * present[c] - earlier(c) + shear * bent[c]


def after_halo(u, metric, lift, bend, base, shear, both, table2, nx, ny, spacing, put):
    inner_x, inner_y = slice(2, 2 + nx), slice(OFF, OFF + ny)
    t1 = 1.0 / (12.0 * spacing)
    t2 = 1.0 / (12.0 * spacing * spacing)

    def first(m2, m1, p1, p2):
        return t1 * ((m2 - p2) + 8.0 * (p1 - m1))

    def second(m2, m1, mid, p1, p2):
        return t2 * (16.0 * (m1 + p1) - (m2 + p2) - 30.0 * mid)

    def along_y(read):
        return [read(slice(OFF + s, OFF + s + ny)) for s in (-2, -1, 0, 1, 2)]

    def along_x(values):
        return [values[2 + s : 2 + s + nx] for s in (-2, -1, 0, 1, 2)]

    layers = u.shape[-1]
    rims = (
        (slice(0, 2), inner_y),
        (slice(2 + nx, 4 + nx), inner_y),
        (inner_x, slice(0, OFF)),
        (inner_x, slice(OFF + ny, 2 * OFF + ny)),
    )
    rows = [u[2, xs, ys].reshape(-1, layers) for xs, ys in rims]
    found = vertical12(jnp.concatenate(rows, axis=0), table2)
    start = 0
    for (xs, ys), part in zip(rims, rows):
        scale = metric[xs, ys] * (1.0 / 12.0)
        lift[xs, ys] = scale * found[start : start + part.shape[0]].reshape(scale.shape)
        start += part.shape[0]

    m2, m1, mid, p1, p2 = along_x(u[0])
    bend[...] = first(m2, m1, p1, p2) + lift[inner_x]
    curve_x0 = second(*[v[:, inner_y] for v in (m2, m1, mid, p1, p2)])
    slope_x0 = bend[:, inner_y]

    m2, m1, mid, p1, p2 = along_y(lambda ys: u[1, :, ys])
    slant = first(m2, m1, p1, p2) + lift[:, inner_y]
    spread = slant[inner_x] + slope_x0 - lift[inner_x, inner_y]
    bent = (metric[inner_x, inner_y] * (1.0 / 12.0)) * vertical12(spread, table2)
    curve_y1 = second(*[v[inner_x] for v in (m2, m1, mid, p1, p2)])
    curve_x1 = second(*along_x(mid))
    m2, m1, _, p1, p2 = along_x(slant)
    graddiv_0 = curve_x0 + first(m2, m1, p1, p2)
    curve_y0 = second(*along_y(lambda ys: u[0, inner_x, ys]))
    put(0, base[0] + shear * (curve_x0 + curve_y0) + both * graddiv_0)

    m2, m1, mid, p1, p2 = along_y(lambda ys: bend[:, ys])
    graddiv_1 = curve_y1 + first(m2, m1, p1, p2)
    put(1, base[1] + shear * (curve_x1 + curve_y1) + both * graddiv_1)

    curve_2 = second(*along_x(u[2, :, inner_y])) + second(*along_y(lambda ys: u[2, inner_x, ys]))
    put(2, base[2] + shear * curve_2 + both * bent)


def kernel(
    size_x,
    size_y,
    fine_now,
    fine_prev,
    coarse_now,
    coarse_prev,
    fine_rho,
    fine_mu,
    fine_lam,
    fine_metric,
    coarse_rho,
    coarse_mu,
    coarse_lam,
    coarse_metric,
    couple_index,
    couple_weight,
    fine_out,
    coarse_out,
    f1,
    f2,
    c1,
    c2,
    f_old,
    c_old,
    f_par,
    c_par,
    index_in,
    weight_in,
    f_lift,
    f_bend,
    c_lift,
    c_bend,
    t2,
    mix,
    table,
    f_base,
    c_base,
    load_sem,
    send_sem,
    recv_sem,
):
    nxf, nyf, layers = fine_rho.shape
    nxc, nyc, _ = coarse_rho.shape
    span = OFF + nyc
    gx, gy = lax.axis_index("gx"), lax.axis_index("gy")

    def inner(nx, ny):
        return pl.ds(2, nx), pl.ds(OFF, ny)

    def exists(dx, dy):
        ok = None
        for step, position, size in ((dx, gx, size_x), (dy, gy, size_y)):
            if step:
                here = position >= 1 if step < 0 else position <= size - 2
                ok = here if ok is None else jnp.logical_and(ok, here)
        return ok

    barrier = pltpu.get_barrier_semaphore()
    for dx, dy in DIRS:

        @pl.when(exists(dx, dy))
        def _():
            pl.semaphore_signal(
                barrier, inc=1, device_id=(gx + dx, gy + dy), device_id_type=MESH
            )

    fx, fy = inner(nxf, nyf)
    cx, cy = inner(nxc, nyc)
    pairs = [
        (coarse_now, c1.at[0:3, cx, cy]),
        (coarse_metric, c1.at[3, cx, cy]),
        (fine_now, f1.at[0:3, fx, fy]),
        (fine_metric, f1.at[3, fx, fy]),
        (coarse_rho, c_par.at[0]),
        (coarse_mu, c_par.at[1]),
        (coarse_lam, c_par.at[2]),
        (coarse_prev, c_old),
        (fine_rho, f_par.at[0]),
        (fine_mu, f_par.at[1]),
        (fine_lam, f_par.at[2]),
        (fine_prev, f_old),
        (couple_index, index_in),
        (couple_weight, weight_in),
    ]
    loads = [
        pltpu.make_async_copy(source, target, load_sem.at[n])
        for n, (source, target) in enumerate(pairs)
    ]
    for load in loads[0:4]:
        load.start()

    def source_range(step, start, length):
        return {-1: pl.ds(start, 2), 1: pl.ds(start + length - 2, 2), 0: pl.ds(start, length)}[step]

    def target_range(step, start, length, wrap=0):
        after = start + length - wrap
        return {-1: pl.ds(after, 2), 1: pl.ds(start - 2, 2), 0: pl.ds(start, length)}[step]

    class Exchange:
        def __init__(self, base, buffer, nx, ny, sides, corners, wrap=0, operand=None):
            self.copies = []
            self.targets = []
            for n, (dx, dy) in enumerate(DIRS):
                parts = sides if n < 4 else corners
                xs, ys = source_range(dx, 2, nx), source_range(dy, OFF, ny)
                xt, yt = target_range(dx, 2, nx), target_range(dy, OFF, ny, wrap)
                if parts is None:
                    src, dst = buffer.at[xs, ys], buffer.at[xt, yt]
                    self.targets.append((buffer, (xt, yt), (xt.size, yt.size, layers)))
                else:
                    ps = parts if isinstance(parts, int) else pl.ds(*parts)
                    src, dst = buffer.at[ps, xs, ys], buffer.at[ps, xt, yt]
                    lead = () if isinstance(parts, int) else (parts[1],)
                    self.targets.append((buffer, (ps, xt, yt), lead + (xt.size, yt.size, layers)))
                    if operand is not None:
                        xo, yo = source_range(dx, 0, nx), source_range(dy, 0, ny)
                        src = operand.at[xo, yo] if isinstance(parts, int) else operand.at[ps, xo, yo]
                copy = pltpu.make_async_remote_copy(
                    src_ref=src,
                    dst_ref=dst,
                    send_sem=send_sem.at[base + n],
                    recv_sem=recv_sem.at[base + n],
                    device_id=(gx + dx, gy + dy),
                    device_id_type=MESH,
                )
                self.copies.append(copy)

        def start(self, which=(4, 5, 6, 7, 0, 1, 2, 3)):
            for n in which:
                pl.when(exists(*DIRS[n]))(self.copies[n].start)

        def arrive(self, which=range(8)):
            for n in which:
                dx, dy = DIRS[n]
                pl.when(exists(-dx, -dy))(self.copies[n].wait_recv)

        def finish(self, which=range(8)):
            for n in which:
                pl.when(exists(*DIRS[n]))(self.copies[n].wait_send)

    whole, pair, sides = (0, 3), (0, 2), range(4)
    coarse_a = Exchange(0, c1, nxc, nyc, whole, pair, operand=coarse_now)
    fine_a = Exchange(8, f1, nxf, nyf, whole, pair, operand=fine_now)
    coarse_b = Exchange(16, c2, nxc, nyc, whole, whole)
    fine_b = Exchange(24, f2, nxf, nyf, whole, pair)
    top_c = Exchange(32, t2, nxc, nyc, None, None, wrap=span)
    coarse_m = Exchange(40, c1, nxc, nyc, 3, 3, operand=coarse_metric)
    fine_m = Exchange(48, f1, nxf, nyf, 3, 3, operand=fine_metric)
    exchanges = (coarse_a, fine_a, coarse_b, fine_b, top_c, coarse_m, fine_m)

    sides_x = 1 + (gx >= 1).astype(jnp.int32) + (gx <= size_x - 2).astype(jnp.int32)
    sides_y = 1 + (gy >= 1).astype(jnp.int32) + (gy <= size_y - 2).astype(jnp.int32)
    pl.semaphore_wait(barrier, sides_x * sides_y - 1)
    coarse_a.start()
    coarse_m.start(sides)
    fine_a.start()
    fine_m.start(sides)
    for load in loads[4:]:
        load.start()
    half = vertical_table12(layers)
    table[...] = jnp.concatenate([half, half], axis=0)

    for n, (dx, dy) in enumerate(DIRS):

        @pl.when(jnp.logical_not(exists(-dx, -dy)))
        def _():
            for exchange in exchanges:
                buffer, where, shape = exchange.targets[n]
                buffer[where] = jnp.zeros(shape, f32)

    cells = (nxc + 4) * span

    def build_mix():
        width = nyc + 4
        reciprocal = (2048 + width - 1) // width
        index = index_in[...].reshape(nxf * nyf, -1)
        weight = weight_in[...].reshape(nxf * nyf, -1)
        row = jnp.right_shift(index * reciprocal, 11)
        column = index - row * width + (OFF - 2)
        column = jnp.where(column >= span, column - span, column)
        place = row * span + column
        cell = lax.broadcasted_iota(jnp.int32, (nxf * nyf, cells), 1)
        total = jnp.zeros((nxf * nyf, cells), f32)
        for j in range(index.shape[1]):
            total += jnp.where(cell == place[:, j : j + 1], weight[:, j : j + 1], 0.0)
        mix_high, mix_low = halves(total)
        mix[0] = mix_high
        mix[1] = mix_low

    lane = lax.broadcasted_iota(jnp.int32, (1, 1, layers), 2)

    def tops(parts):
        out = None
        for c, values in enumerate(parts):
            only = jnp.where(lane == layers - 1, values, 0.0)
            moved = pltpu.roll(only.reshape(-1, layers), c + 1, 1).reshape(values.shape)
            out = moved if out is None else out + moved
        return out

    def interface(top, parts):
        high, low = halves(top.reshape(cells, layers))
        found = dot(mix[0], high) + (dot(mix[1], high) + dot(mix[0], low))
        result = []
        for c, values in enumerate(parts):
            moved = found if c == 0 else pltpu.roll(found, layers - c, 1)
            result.append(jnp.where(lane == 0, moved.reshape(values.shape), values))
        return result

    f_in = (slice(2, 2 + nxf), slice(OFF, OFF + nyf))
    c_in = (slice(2, 2 + nxc), slice(OFF, OFF + nyc))

    def parameters(par):
        scale = (time_step * time_step) / par[0]
        shear = par[1]
        par[0] = shear * scale
        par[1] = (par[2] + shear) * scale

    def fine_before(u, earlier):
        before_halo(u, f1.at[3], f_lift, f_base, earlier, f_par[0], table[...], nxf, nyf)

    def coarse_before(u, earlier):
        before_halo(u, c1.at[3], c_lift, c_base, earlier, c_par[0], table[...], nxc, nyc)

    def fine_after(u, put):
        after_halo(
            u, f1.at[3], f_lift, f_bend, f_base, f_par[0], f_par[1], table[...], nxf, nyf, 1.0, put
        )

    def coarse_after(u, put):
        after_halo(
            u, c1.at[3], c_lift, c_bend, c_base, c_par[0], c_par[1], table[...], nxc, nyc, 2.0, put
        )

    def put_in(buffer, where):
        def put(c, values):
            buffer[c, where[0], where[1]] = values

        return put

    def put_out(buffer):
        def put(c, values):
            buffer[c] = values

        return put

    for load in (loads[0], loads[1], *loads[4:8]):
        load.wait()
    parameters(c_par)
    coarse_before(c1, lambda c: c_old[c])
    for load in (loads[2], loads[3], *loads[8:12]):
        load.wait()
    parameters(f_par)
    fine_before(f1, lambda c: f_old[c])
    coarse_a.arrive()
    coarse_m.arrive(sides)
    coarse_after(c1, put_in(c2, c_in))
    coarse_b.start()
    fine_a.arrive()
    fine_m.arrive(sides)
    fine_after(f1, put_in(f2, f_in))
    for load in loads[12:]:
        load.wait()
    build_mix()
    coarse_before(c2, lambda c: c1[c, c_in[0], c_in[1]])
    for exchange, which in ((coarse_a, range(8)), (fine_a, range(8)), (coarse_m, sides), (fine_m, sides)):
        exchange.finish(which)
    coarse_b.arrive()
    sub = lax.broadcasted_iota(jnp.int32, (1, OFF, 1), 1)
    rims = []
    for c in range(3):
        after, before = c2[c, :, OFF + nyc : 2 * OFF + nyc], c2[c, :, 0:OFF]
        rims.append(jnp.where(sub < 2, after, jnp.where(sub >= OFF - 2, before, 0.0)))
    top = jnp.concatenate([tops(rims), tops([c2[c, :, c_in[1]] for c in range(3)])], axis=1)
    for c, values in enumerate(interface(top, [f2[c, f_in[0], f_in[1]] for c in range(3)])):
        f2[c, f_in[0], f_in[1]] = values
    fine_b.start()

    coarse_after(c2, put_out(coarse_out))
    t2[c_in[0], c_in[1]] = tops([coarse_out[c] for c in range(3)])
    top_c.start()
    fine_before(f2, lambda c: f1[c, f_in[0], f_in[1]])
    coarse_b.finish()
    fine_b.arrive()
    fine_after(f2, put_out(fine_out))
    fine_b.finish()
    top_c.arrive()
    rim = jnp.where(jnp.logical_or(sub < 2, sub >= OFF - 2), t2[:, 0:OFF], 0.0)
    top = jnp.concatenate([rim, t2[:, OFF:span]], axis=1)
    for c, values in enumerate(interface(top, [fine_out[c] for c in range(3)])):
        fine_out[c] = values
    top_c.finish()


def finish(fine_in, coarse_in, fine_out, coarse_out, sem):
    copies = [
        pltpu.make_async_copy(fine_in, fine_out, sem.at[0]),
        pltpu.make_async_copy(coarse_in, coarse_out, sem.at[1]),
    ]
    for copy in copies:
        copy.start()
    for copy in copies:
        copy.wait()


def solution(mesh):
    size_x, size_y = mesh.shape["gx"], mesh.shape["gy"]

    def on_device(*args):
        fine, coarse = args[0], args[2]
        _, nxf, nyf, layers = fine.shape
        _, nxc, nyc, _ = coarse.shape
        index = args[12]

        def wide(parts, nx, ny):
            return pltpu.VMEM((parts, nx + 4, ny + 2 * OFF, layers), f32)

        span = OFF + nyc
        scratch = [
            wide(4, nxf, nyf),
            wide(3, nxf, nyf),
            wide(4, nxc, nyc),
            wide(3, nxc, nyc),
            pltpu.VMEM(fine.shape, f32),
            pltpu.VMEM(coarse.shape, f32),
            pltpu.VMEM(fine.shape, f32),
            pltpu.VMEM(coarse.shape, f32),
            pltpu.VMEM(index.shape, jnp.int32),
            pltpu.VMEM(index.shape, f32),
            pltpu.VMEM((nxf + 4, nyf + 2 * OFF, layers), f32),
            pltpu.VMEM((nxf, nyf + 2 * OFF, layers), f32),
            pltpu.VMEM((nxc + 4, nyc + 2 * OFF, layers), f32),
            pltpu.VMEM((nxc, nyc + 2 * OFF, layers), f32),
            pltpu.VMEM((nxc + 4, span, layers), f32),
            pltpu.VMEM((2, nxf * nyf, (nxc + 4) * span), bf16),
            pltpu.VMEM((2 * layers, layers), bf16),
            pltpu.VMEM(fine.shape, f32),
            pltpu.VMEM(coarse.shape, f32),
            pltpu.SemaphoreType.DMA((14,)),
            pltpu.SemaphoreType.DMA((56,)),
            pltpu.SemaphoreType.DMA((56,)),
        ]
        shapes = (
            jax.ShapeDtypeStruct(fine.shape, f32),
            jax.ShapeDtypeStruct(coarse.shape, f32),
        )
        hbm, vmem = pl.BlockSpec(memory_space=pltpu.HBM), pl.BlockSpec(memory_space=pltpu.VMEM)
        args = [pltpu.with_memory_space_constraint(arg, pltpu.HBM) for arg in args]
        results = pl.pallas_call(
            functools.partial(kernel, size_x, size_y),
            out_shape=(pltpu.VMEM(fine.shape, f32), pltpu.VMEM(coarse.shape, f32)),
            in_specs=[hbm] * 14,
            out_specs=(vmem, vmem),
            scratch_shapes=scratch,
            compiler_params=pltpu.CompilerParams(
                collective_id=0, has_side_effects=True, vmem_limit_bytes=32 * 1024 * 1024
            ),
        )(*args)
        return pl.pallas_call(
            finish,
            out_shape=shapes,
            in_specs=[vmem, vmem],
            out_specs=(hbm, hbm),
            scratch_shapes=[pltpu.SemaphoreType.DMA((2,))],
            compiler_params=pltpu.CompilerParams(vmem_limit_bytes=16 * 1024 * 1024),
        )(*results)

    field, flat = P(None, "gx", "gy", None), P("gx", "gy", None)
    return jax.shard_map(
        on_device,
        mesh=mesh,
        in_specs=(field,) * 4 + (flat,) * 10,
        out_specs=(field, field),
        check_vma=False,
    )
```

```python
import functools

import jax
import jax.numpy as jnp
from jax import lax
from jax.experimental import pallas as pl
from jax.experimental.pallas import tpu as pltpu
from jax.sharding import PartitionSpec as P

MESH = pl.DeviceIdType.MESH
f32 = jnp.float32
bf16 = jnp.bfloat16
time_step = 0.25
OFF = 8
SIDES = ((-1, 0), (1, 0), (0, -1), (0, 1))
CORNERS = ((-1, -1), (-1, 1), (1, -1), (1, 1))
DIRS = SIDES + CORNERS


def vertical_table12(layers):
    level_in = lax.broadcasted_iota(jnp.int32, (layers, layers), 0)
    level_out = lax.broadcasted_iota(jnp.int32, (layers, layers), 1)
    apart = level_in - level_out
    table = jnp.where(apart == -2, 1.0, 0.0)
    table = jnp.where(apart == -1, -8.0, table)
    table = jnp.where(apart == 1, 8.0, table)
    table = jnp.where(apart == 2, -1.0, table)
    last = layers - 1
    edges = {
        0: ((0, -18.0), (1, 24.0), (2, -6.0)),
        1: ((0, -6.0), (2, 6.0)),
        last - 1: ((last - 2, -6.0), (last, 6.0)),
        last: ((last - 2, 6.0), (last - 1, -24.0), (last, 18.0)),
    }
    for row, taps in edges.items():
        column = jnp.zeros_like(table)
        for level, value in taps:
            column = jnp.where(level_in == level, value, column)
        table = jnp.where(level_out == row, column, table)
    return table.astype(bf16)


def halves(values):
    high = values.astype(bf16)
    low = (values - high.astype(f32)).astype(bf16)
    return high, low


def dot(left, right):
    return jnp.dot(left, right, preferred_element_type=f32)


def vertical12(values, table2):
    shape = values.shape
    high, low = halves(values.reshape(-1, shape[-1]))
    return dot(jnp.concatenate([high, low], axis=1), table2).reshape(shape)


def before_halo(u, metric, lift, base, earlier, shear, table2, nx, ny):
    inner_x, inner_y = slice(2, 2 + nx), slice(OFF, OFF + ny)
    metric_in = metric[inner_x, inner_y] * (1.0 / 12.0)
    slopes = [metric_in * vertical12(u[c, inner_x, inner_y], table2) for c in range(3)]
    lift[inner_x, inner_y] = slopes[2]
    for c in range(3):
        bent = metric_in * vertical12(slopes[c], table2)
        base[c] = 2.0 * u[c, inner_x, inner_y] - earlier(c) + shear[...] * bent


def after_halo(u, metric, lift, bend, base, shear, both, table2, nx, ny, spacing, put):
    inner_x, inner_y = slice(2, 2 + nx), slice(OFF, OFF + ny)
    t1 = 1.0 / (12.0 * spacing)
    t2 = 1.0 / (12.0 * spacing * spacing)
    taps = (-2, -1, 1, 2)

    def first(m2, m1, p1, p2):
        return t1 * (m2 - p2) + (8.0 * t1) * (p1 - m1)

    def pairs(m2, m1, p1, p2):
        return m1 + p1, m2 + p2

    def second(near, far, mid, weight):
        return (16.0 * t2) * near - t2 * far - (weight * t2) * mid

    def shifted(read):
        return [read(slice(OFF + s, OFF + s + ny)) for s in taps]

    layers = u.shape[-1]
    rims = (
        (slice(0, 2), inner_y),
        (slice(2 + nx, 4 + nx), inner_y),
        (inner_x, slice(0, OFF)),
        (inner_x, slice(OFF + ny, 2 * OFF + ny)),
    )
    for xs, ys in rims:
        lift[xs, ys] = (metric[xs, ys] * (1.0 / 12.0)) * vertical12(u[2, xs, ys], table2)

    slants, sums = [], []
    for row in range(nx + 4):
        near_y = shifted(lambda ys: u[1, row, ys])
        slants.append(first(*near_y) + lift[row, inner_y])
        sums.append(pairs(*near_y))
        i = row - 4
        if i < 0:
            continue
        m = i + 2
        wide = [u[0, m + s] for s in taps]
        bend[i] = first(*wide) + lift[m]
        near, far = pairs(*[v[inner_y] for v in wide])
        mid = u[0, m, inner_y]
        curve_x = second(near, far, mid, 30.0)
        near, far = pairs(*shifted(lambda ys: u[0, m, ys]))
        curve = curve_x + second(near, far, mid, 30.0)
        graddiv = curve_x + first(*[slants[m + s] for s in taps])
        put(0, i, base[0, i] + shear[i] * curve + both[i] * graddiv)
        near, far = sums[m]
        mid = u[1, m, inner_y]
        curve_y = second(near, far, mid, 30.0)
        near, far = pairs(*[u[1, m + s, inner_y] for s in taps])
        curve = curve_y + second(near, far, mid, 30.0)
        graddiv = curve_y + first(*shifted(lambda ys: bend[i, ys]))
        put(1, i, base[1, i] + shear[i] * curve + both[i] * graddiv)
        near, far = pairs(*[u[2, m + s, inner_y] for s in taps])
        near_y, far_y = pairs(*shifted(lambda ys: u[2, m, ys]))
        curve = second(near + near_y, far + far_y, u[2, m, inner_y], 60.0)
        base[2, i] = base[2, i] + shear[i] * curve
        base[0, i] = slants[m] + (bend[i, inner_y] - lift[m, inner_y])

    bent = (metric[inner_x, inner_y] * (1.0 / 12.0)) * vertical12(base[0], table2)
    for i in range(nx):
        put(2, i, base[2, i] + both[i] * bent[i])


def kernel(
    size_x,
    size_y,
    fine_now,
    fine_prev,
    coarse_now,
    coarse_prev,
    fine_rho,
    fine_mu,
    fine_lam,
    fine_metric,
    coarse_rho,
    coarse_mu,
    coarse_lam,
    coarse_metric,
    couple_index,
    couple_weight,
    fine_out,
    coarse_out,
    f1,
    f2,
    c1,
    c2,
    f_old,
    c_old,
    f_par,
    c_par,
    index_in,
    weight_in,
    f_lift,
    f_bend,
    c_lift,
    c_bend,
    t2,
    mix,
    table,
    f_base,
    c_base,
    load_sem,
    send_sem,
    recv_sem,
):
    nxf, nyf, layers = fine_rho.shape
    nxc, nyc, _ = coarse_rho.shape
    span = OFF + nyc
    gx, gy = lax.axis_index("gx"), lax.axis_index("gy")

    def inner(nx, ny):
        return pl.ds(2, nx), pl.ds(OFF, ny)

    def exists(dx, dy):
        ok = None
        for step, position, size in ((dx, gx, size_x), (dy, gy, size_y)):
            if step:
                here = position >= 1 if step < 0 else position <= size - 2
                ok = here if ok is None else jnp.logical_and(ok, here)
        return ok

    barrier = pltpu.get_barrier_semaphore()
    for dx, dy in DIRS:

        @pl.when(exists(dx, dy))
        def _():
            pl.semaphore_signal(
                barrier, inc=1, device_id=(gx + dx, gy + dy), device_id_type=MESH
            )

    fx, fy = inner(nxf, nyf)
    cx, cy = inner(nxc, nyc)
    pairs = [
        (coarse_now, c1.at[0:3, cx, cy]),
        (coarse_metric, c1.at[3, cx, cy]),
        (fine_now, f1.at[0:3, fx, fy]),
        (fine_metric, f1.at[3, fx, fy]),
        (coarse_rho, c_par.at[0]),
        (coarse_mu, c_par.at[1]),
        (coarse_lam, c_par.at[2]),
        (coarse_prev, c_old),
        (fine_rho, f_par.at[0]),
        (fine_mu, f_par.at[1]),
        (fine_lam, f_par.at[2]),
        (fine_prev, f_old),
        (couple_index, index_in),
        (couple_weight, weight_in),
    ]
    loads = [
        pltpu.make_async_copy(source, target, load_sem.at[n])
        for n, (source, target) in enumerate(pairs)
    ]
    for load in loads:
        load.start()

    half = vertical_table12(layers)
    table[...] = jnp.concatenate([half, half], axis=0)

    def source_range(step, start, length):
        return {-1: pl.ds(start, 2), 1: pl.ds(start + length - 2, 2), 0: pl.ds(start, length)}[step]

    def target_range(step, start, length, wrap=0):
        after = start + length - wrap
        return {-1: pl.ds(after, 2), 1: pl.ds(start - 2, 2), 0: pl.ds(start, length)}[step]

    class Exchange:
        def __init__(self, base, buffer, nx, ny, sides, corners, wrap=0):
            self.copies = []
            self.targets = []
            for n, (dx, dy) in enumerate(DIRS):
                parts = sides if n < 4 else corners
                xs, ys = source_range(dx, 2, nx), source_range(dy, OFF, ny)
                xt, yt = target_range(dx, 2, nx), target_range(dy, OFF, ny, wrap)
                if parts is None:
                    src, dst = buffer.at[xs, ys], buffer.at[xt, yt]
                    self.targets.append((buffer, (xt, yt), (xt.size, yt.size, layers)))
                else:
                    ps = pl.ds(0, parts)
                    src, dst = buffer.at[ps, xs, ys], buffer.at[ps, xt, yt]
                    self.targets.append((buffer, (ps, xt, yt), (parts, xt.size, yt.size, layers)))
                copy = pltpu.make_async_remote_copy(
                    src_ref=src,
                    dst_ref=dst,
                    send_sem=send_sem.at[base + n],
                    recv_sem=recv_sem.at[base + n],
                    device_id=(gx + dx, gy + dy),
                    device_id_type=MESH,
                )
                self.copies.append(copy)

        def start(self):
            for n in (4, 5, 6, 7, 0, 1, 2, 3):
                pl.when(exists(*DIRS[n]))(self.copies[n].start)

        def arrive(self):
            for (dx, dy), copy in zip(DIRS, self.copies):
                pl.when(exists(-dx, -dy))(copy.wait_recv)

        def finish(self):
            for (dx, dy), copy in zip(DIRS, self.copies):
                pl.when(exists(dx, dy))(copy.wait_send)

    coarse_a = Exchange(0, c1, nxc, nyc, 4, 2)
    fine_a = Exchange(8, f1, nxf, nyf, 4, 2)
    coarse_b = Exchange(16, c2, nxc, nyc, 3, 3)
    fine_b = Exchange(24, f2, nxf, nyf, 3, 2)
    top_c = Exchange(32, t2, nxc, nyc, None, None, wrap=span)
    exchanges = (coarse_a, fine_a, coarse_b, fine_b, top_c)

    for load in loads[0:4]:
        load.wait()
    sides_x = 1 + (gx >= 1).astype(jnp.int32) + (gx <= size_x - 2).astype(jnp.int32)
    sides_y = 1 + (gy >= 1).astype(jnp.int32) + (gy <= size_y - 2).astype(jnp.int32)
    pl.semaphore_wait(barrier, sides_x * sides_y - 1)
    coarse_a.start()
    fine_a.start()

    for n, (dx, dy) in enumerate(DIRS):

        @pl.when(jnp.logical_not(exists(-dx, -dy)))
        def _():
            for exchange in exchanges:
                buffer, where, shape = exchange.targets[n]
                buffer[where] = jnp.zeros(shape, f32)

    cells = (nxc + 4) * span

    def build_mix():
        width = nyc + 4
        reciprocal = (2048 + width - 1) // width
        planes = max(1, 32 // nyf)
        rows = planes * nyf
        cell = lax.broadcasted_iota(jnp.int32, (rows, cells), 1)
        for part in range(nxf // planes):
            here = slice(part * planes, (part + 1) * planes)
            index = index_in[here].reshape(rows, -1)
            weight = weight_in[here].reshape(rows, -1)
            row = jnp.right_shift(index * reciprocal, 11)
            column = index - row * width + (OFF - 2)
            column = jnp.where(column >= span, column - span, column)
            place = row * span + column
            total = jnp.zeros((rows, cells), f32)
            for j in range(index.shape[1]):
                total += jnp.where(cell == place[:, j : j + 1], weight[:, j : j + 1], 0.0)
            mix_high, mix_low = halves(total)
            mix[0, part * rows : (part + 1) * rows] = mix_high
            mix[1, part * rows : (part + 1) * rows] = mix_low

    lane = lax.broadcasted_iota(jnp.int32, (1, 1, layers), 2)

    def tops(parts):
        out = None
        for c, values in enumerate(parts):
            only = jnp.where(lane == layers - 1, values, 0.0)
            moved = pltpu.roll(only.reshape(-1, layers), c + 1, 1).reshape(values.shape)
            out = moved if out is None else out + moved
        return out

    def interface(top, parts):
        high, low = halves(top.reshape(cells, layers))
        found = dot(mix[0], high) + (dot(mix[1], high) + dot(mix[0], low))
        result = []
        for c, values in enumerate(parts):
            moved = found if c == 0 else pltpu.roll(found, layers - c, 1)
            result.append(jnp.where(lane == 0, moved.reshape(values.shape), values))
        return result

    f_in = (slice(2, 2 + nxf), slice(OFF, OFF + nyf))
    c_in = (slice(2, 2 + nxc), slice(OFF, OFF + nyc))

    def parameters(par):
        scale = (time_step * time_step) / par[0]
        shear = par[1]
        par[0] = shear * scale
        par[1] = (par[2] + shear) * scale

    def fine_before(u, earlier):
        before_halo(u, f1.at[3], f_lift, f_base, earlier, f_par.at[0], table[...], nxf, nyf)

    def coarse_before(u, earlier):
        before_halo(u, c1.at[3], c_lift, c_base, earlier, c_par.at[0], table[...], nxc, nyc)

    def fine_after(u, put):
        after_halo(
            u, f1.at[3], f_lift, f_bend, f_base, f_par.at[0], f_par.at[1], table[...], nxf, nyf, 1.0, put
        )

    def coarse_after(u, put):
        after_halo(
            u, c1.at[3], c_lift, c_bend, c_base, c_par.at[0], c_par.at[1], table[...], nxc, nyc, 2.0, put
        )

    def put_in(buffer, where):
        def put(c, row, values):
            buffer[c, where[0].start + row, where[1]] = values

        return put

    def put_out(buffer):
        def put(c, row, values):
            buffer[c, row] = values

        return put

    for load in loads[4:8]:
        load.wait()
    parameters(c_par)
    coarse_before(c1, lambda c: c_old[c])
    coarse_a.arrive()
    coarse_after(c1, put_in(c2, c_in))
    coarse_b.start()
    for load in loads[8:12]:
        load.wait()
    parameters(f_par)
    fine_before(f1, lambda c: f_old[c])
    for load in loads[12:]:
        load.wait()
    build_mix()
    fine_a.arrive()
    fine_after(f1, put_in(f2, f_in))
    coarse_b.arrive()
    sub = lax.broadcasted_iota(jnp.int32, (1, OFF, 1), 1)
    rims = []
    for c in range(3):
        after, before = c2[c, :, OFF + nyc : 2 * OFF + nyc], c2[c, :, 0:OFF]
        rims.append(jnp.where(sub < 2, after, jnp.where(sub >= OFF - 2, before, 0.0)))
    top = jnp.concatenate([tops(rims), tops([c2[c, :, c_in[1]] for c in range(3)])], axis=1)
    for c, values in enumerate(interface(top, [f2[c, f_in[0], f_in[1]] for c in range(3)])):
        f2[c, f_in[0], f_in[1]] = values
    fine_b.start()

    coarse_before(c2, lambda c: c1[c, c_in[0], c_in[1]])
    coarse_after(c2, put_out(coarse_out))
    t2[c_in[0], c_in[1]] = tops([coarse_out[c] for c in range(3)])
    top_c.start()
    fine_before(f2, lambda c: f1[c, f_in[0], f_in[1]])
    fine_b.arrive()
    fine_after(f2, put_out(fine_out))
    top_c.arrive()
    rim = jnp.where(jnp.logical_or(sub < 2, sub >= OFF - 2), t2[:, 0:OFF], 0.0)
    top = jnp.concatenate([rim, t2[:, OFF:span]], axis=1)
    for c, values in enumerate(interface(top, [fine_out[c] for c in range(3)])):
        fine_out[c] = values
    for exchange in exchanges:
        exchange.finish()


def finish(fine_in, coarse_in, fine_out, coarse_out, sem):
    copies = [
        pltpu.make_async_copy(fine_in, fine_out, sem.at[0]),
        pltpu.make_async_copy(coarse_in, coarse_out, sem.at[1]),
    ]
    for copy in copies:
        copy.start()
    for copy in copies:
        copy.wait()


def solution(mesh):
    size_x, size_y = mesh.shape["gx"], mesh.shape["gy"]

    def on_device(*args):
        fine, coarse = args[0], args[2]
        _, nxf, nyf, layers = fine.shape
        _, nxc, nyc, _ = coarse.shape
        index = args[12]

        def wide(parts, nx, ny):
            return pltpu.VMEM((parts, nx + 4, ny + 2 * OFF, layers), f32)

        span = OFF + nyc
        scratch = [
            wide(4, nxf, nyf),
            wide(3, nxf, nyf),
            wide(4, nxc, nyc),
            wide(3, nxc, nyc),
            pltpu.VMEM(fine.shape, f32),
            pltpu.VMEM(coarse.shape, f32),
            pltpu.VMEM(fine.shape, f32),
            pltpu.VMEM(coarse.shape, f32),
            pltpu.VMEM(index.shape, jnp.int32),
            pltpu.VMEM(index.shape, f32),
            pltpu.VMEM((nxf + 4, nyf + 2 * OFF, layers), f32),
            pltpu.VMEM((nxf, nyf + 2 * OFF, layers), f32),
            pltpu.VMEM((nxc + 4, nyc + 2 * OFF, layers), f32),
            pltpu.VMEM((nxc, nyc + 2 * OFF, layers), f32),
            pltpu.VMEM((nxc + 4, span, layers), f32),
            pltpu.VMEM((2, nxf * nyf, (nxc + 4) * span), bf16),
            pltpu.VMEM((2 * layers, layers), bf16),
            pltpu.VMEM(fine.shape, f32),
            pltpu.VMEM(coarse.shape, f32),
            pltpu.SemaphoreType.DMA((14,)),
            pltpu.SemaphoreType.DMA((40,)),
            pltpu.SemaphoreType.DMA((40,)),
        ]
        shapes = (
            jax.ShapeDtypeStruct(fine.shape, f32),
            jax.ShapeDtypeStruct(coarse.shape, f32),
        )
        hbm, vmem = pl.BlockSpec(memory_space=pltpu.HBM), pl.BlockSpec(memory_space=pltpu.VMEM)
        args = [pltpu.with_memory_space_constraint(arg, pltpu.HBM) for arg in args]
        results = pl.pallas_call(
            functools.partial(kernel, size_x, size_y),
            out_shape=(pltpu.VMEM(fine.shape, f32), pltpu.VMEM(coarse.shape, f32)),
            in_specs=[hbm] * 14,
            out_specs=(vmem, vmem),
            scratch_shapes=scratch,
            compiler_params=pltpu.CompilerParams(
                collective_id=0, has_side_effects=True, vmem_limit_bytes=32 * 1024 * 1024
            ),
        )(*args)
        return pl.pallas_call(
            finish,
            out_shape=shapes,
            in_specs=[vmem, vmem],
            out_specs=(hbm, hbm),
            scratch_shapes=[pltpu.SemaphoreType.DMA((2,))],
            compiler_params=pltpu.CompilerParams(vmem_limit_bytes=16 * 1024 * 1024),
        )(*results)

    field, flat = P(None, "gx", "gy", None), P("gx", "gy", None)
    return jax.shard_map(
        on_device,
        mesh=mesh,
        in_specs=(field,) * 4 + (flat,) * 10,
        out_specs=(field, field),
        check_vma=False,
    )
```

```python
import functools

import jax
import jax.numpy as jnp
from jax import lax
from jax.experimental import pallas as pl
from jax.experimental.pallas import tpu as pltpu
from jax.sharding import PartitionSpec as P

MESH = pl.DeviceIdType.MESH
f32 = jnp.float32
bf16 = jnp.bfloat16
time_step = 0.25
OFF = 8
SIDES = ((-1, 0), (1, 0), (0, -1), (0, 1))
CORNERS = ((-1, -1), (-1, 1), (1, -1), (1, 1))
DIRS = SIDES + CORNERS


def vertical_table12(layers):
    level_in = lax.broadcasted_iota(jnp.int32, (layers, layers), 0)
    level_out = lax.broadcasted_iota(jnp.int32, (layers, layers), 1)
    apart = level_in - level_out
    table = jnp.where(apart == -2, 1.0, 0.0)
    table = jnp.where(apart == -1, -8.0, table)
    table = jnp.where(apart == 1, 8.0, table)
    table = jnp.where(apart == 2, -1.0, table)
    last = layers - 1
    edges = {
        0: ((0, -18.0), (1, 24.0), (2, -6.0)),
        1: ((0, -6.0), (2, 6.0)),
        last - 1: ((last - 2, -6.0), (last, 6.0)),
        last: ((last - 2, 6.0), (last - 1, -24.0), (last, 18.0)),
    }
    for row, taps in edges.items():
        column = jnp.zeros_like(table)
        for level, value in taps:
            column = jnp.where(level_in == level, value, column)
        table = jnp.where(level_out == row, column, table)
    return table.astype(bf16)


def halves(values):
    high = values.astype(bf16)
    low = (values - high.astype(f32)).astype(bf16)
    return high, low


def dot(left, right):
    return jnp.dot(left, right, preferred_element_type=f32)


def vertical12(values, table2):
    shape = values.shape
    high, low = halves(values.reshape(-1, shape[-1]))
    return dot(jnp.concatenate([high, low], axis=1), table2).reshape(shape)


def before_halo(u, metric, lift, base, earlier, shear, table2, nx, ny):
    inner_x, inner_y = slice(2, 2 + nx), slice(OFF, OFF + ny)
    metric_in = metric[inner_x, inner_y] * (1.0 / 12.0)
    slopes = [metric_in * vertical12(u[c, inner_x, inner_y], table2) for c in range(3)]
    lift[inner_x, inner_y] = slopes[2]
    for c in range(3):
        bent = metric_in * vertical12(slopes[c], table2)
        base[c] = 2.0 * u[c, inner_x, inner_y] - earlier(c) + shear[...] * bent


def after_halo(u, metric, lift, bend, base, shear, both, table2, nx, ny, spacing, put):
    inner_x, inner_y = slice(2, 2 + nx), slice(OFF, OFF + ny)
    t1 = 1.0 / (12.0 * spacing)
    t2 = 1.0 / (12.0 * spacing * spacing)
    taps = (-2, -1, 1, 2)

    def first(m2, m1, p1, p2):
        return t1 * (m2 - p2) + (8.0 * t1) * (p1 - m1)

    def pairs(m2, m1, p1, p2):
        return m1 + p1, m2 + p2

    def second(near, far, mid, weight):
        return (16.0 * t2) * near - t2 * far - (weight * t2) * mid

    def shifted(read):
        return [read(slice(OFF + s, OFF + s + ny)) for s in taps]

    layers = u.shape[-1]
    rims = (
        (slice(0, 2), inner_y),
        (slice(2 + nx, 4 + nx), inner_y),
        (inner_x, slice(0, OFF)),
        (inner_x, slice(OFF + ny, 2 * OFF + ny)),
    )
    for xs, ys in rims:
        lift[xs, ys] = (metric[xs, ys] * (1.0 / 12.0)) * vertical12(u[2, xs, ys], table2)

    slants, sums = [], []
    for row in range(nx + 4):
        near_y = shifted(lambda ys: u[1, row, ys])
        slants.append(first(*near_y) + lift[row, inner_y])
        sums.append(pairs(*near_y))
        i = row - 4
        if i < 0:
            continue
        m = i + 2
        wide = [u[0, m + s] for s in taps]
        bend[i] = first(*wide) + lift[m]
        near, far = pairs(*[v[inner_y] for v in wide])
        mid = u[0, m, inner_y]
        curve_x = second(near, far, mid, 30.0)
        near, far = pairs(*shifted(lambda ys: u[0, m, ys]))
        curve = curve_x + second(near, far, mid, 30.0)
        graddiv = curve_x + first(*[slants[m + s] for s in taps])
        put(0, i, base[0, i] + shear[i] * curve + both[i] * graddiv)
        near, far = sums[m]
        mid = u[1, m, inner_y]
        curve_y = second(near, far, mid, 30.0)
        near, far = pairs(*[u[1, m + s, inner_y] for s in taps])
        curve = curve_y + second(near, far, mid, 30.0)
        graddiv = curve_y + first(*shifted(lambda ys: bend[i, ys]))
        put(1, i, base[1, i] + shear[i] * curve + both[i] * graddiv)
        near, far = pairs(*[u[2, m + s, inner_y] for s in taps])
        near_y, far_y = pairs(*shifted(lambda ys: u[2, m, ys]))
        curve = second(near + near_y, far + far_y, u[2, m, inner_y], 60.0)
        base[2, i] = base[2, i] + shear[i] * curve
        base[0, i] = slants[m] + (bend[i, inner_y] - lift[m, inner_y])

    bent = (metric[inner_x, inner_y] * (1.0 / 12.0)) * vertical12(base[0], table2)
    for i in range(nx):
        put(2, i, base[2, i] + both[i] * bent[i])


def kernel(
    size_x,
    size_y,
    fine_now,
    fine_prev,
    coarse_now,
    coarse_prev,
    fine_rho,
    fine_mu,
    fine_lam,
    fine_metric,
    coarse_rho,
    coarse_mu,
    coarse_lam,
    coarse_metric,
    couple_index,
    couple_weight,
    fine_out,
    coarse_out,
    f1,
    f2,
    c1,
    c2,
    f_old,
    c_old,
    f_par,
    c_par,
    index_in,
    weight_in,
    f_lift,
    f_bend,
    c_lift,
    c_bend,
    t2,
    mix,
    table,
    f_base,
    c_base,
    load_sem,
    send_sem,
    recv_sem,
):
    nxf, nyf, layers = fine_rho.shape
    nxc, nyc, _ = coarse_rho.shape
    span = OFF + nyc
    gx, gy = lax.axis_index("gx"), lax.axis_index("gy")

    def inner(nx, ny):
        return pl.ds(2, nx), pl.ds(OFF, ny)

    def exists(dx, dy):
        ok = None
        for step, position, size in ((dx, gx, size_x), (dy, gy, size_y)):
            if step:
                here = position >= 1 if step < 0 else position <= size - 2
                ok = here if ok is None else jnp.logical_and(ok, here)
        return ok

    barrier = pltpu.get_barrier_semaphore()
    for dx, dy in DIRS:

        @pl.when(exists(dx, dy))
        def _():
            pl.semaphore_signal(
                barrier, inc=1, device_id=(gx + dx, gy + dy), device_id_type=MESH
            )

    fx, fy = inner(nxf, nyf)
    cx, cy = inner(nxc, nyc)
    pairs = [
        (coarse_now, c1.at[0:3, cx, cy]),
        (coarse_metric, c1.at[3, cx, cy]),
        (fine_now, f1.at[0:3, fx, fy]),
        (fine_metric, f1.at[3, fx, fy]),
        (coarse_rho, c_par.at[0]),
        (coarse_mu, c_par.at[1]),
        (coarse_lam, c_par.at[2]),
        (coarse_prev, c_old),
        (fine_rho, f_par.at[0]),
        (fine_mu, f_par.at[1]),
        (fine_lam, f_par.at[2]),
        (fine_prev, f_old),
        (couple_index, index_in),
        (couple_weight, weight_in),
    ]
    loads = [
        pltpu.make_async_copy(source, target, load_sem.at[n])
        for n, (source, target) in enumerate(pairs)
    ]
    for load in loads[0:4]:
        load.start()

    def source_range(step, start, length):
        return {-1: pl.ds(start, 2), 1: pl.ds(start + length - 2, 2), 0: pl.ds(start, length)}[step]

    def target_range(step, start, length, wrap=0):
        after = start + length - wrap
        return {-1: pl.ds(after, 2), 1: pl.ds(start - 2, 2), 0: pl.ds(start, length)}[step]

    class Exchange:
        def __init__(self, base, buffer, nx, ny, sides, corners, wrap=0):
            self.copies = []
            self.targets = []
            for n, (dx, dy) in enumerate(DIRS):
                parts = sides if n < 4 else corners
                xs, ys = source_range(dx, 2, nx), source_range(dy, OFF, ny)
                xt, yt = target_range(dx, 2, nx), target_range(dy, OFF, ny, wrap)
                if parts is None:
                    src, dst = buffer.at[xs, ys], buffer.at[xt, yt]
                    self.targets.append((buffer, (xt, yt), (xt.size, yt.size, layers)))
                else:
                    ps = pl.ds(0, parts)
                    src, dst = buffer.at[ps, xs, ys], buffer.at[ps, xt, yt]
                    self.targets.append((buffer, (ps, xt, yt), (parts, xt.size, yt.size, layers)))
                copy = pltpu.make_async_remote_copy(
                    src_ref=src,
                    dst_ref=dst,
                    send_sem=send_sem.at[base + n],
                    recv_sem=recv_sem.at[base + n],
                    device_id=(gx + dx, gy + dy),
                    device_id_type=MESH,
                )
                self.copies.append(copy)

        def start(self):
            for n in (4, 5, 6, 7, 0, 1, 2, 3):
                pl.when(exists(*DIRS[n]))(self.copies[n].start)

        def arrive(self):
            for (dx, dy), copy in zip(DIRS, self.copies):
                pl.when(exists(-dx, -dy))(copy.wait_recv)

        def finish(self):
            for (dx, dy), copy in zip(DIRS, self.copies):
                pl.when(exists(dx, dy))(copy.wait_send)

    coarse_a = Exchange(0, c1, nxc, nyc, 4, 2)
    fine_a = Exchange(8, f1, nxf, nyf, 4, 2)
    coarse_b = Exchange(16, c2, nxc, nyc, 3, 3)
    fine_b = Exchange(24, f2, nxf, nyf, 3, 2)
    top_c = Exchange(32, t2, nxc, nyc, None, None, wrap=span)
    exchanges = (coarse_a, fine_a, coarse_b, fine_b, top_c)

    sides_x = 1 + (gx >= 1).astype(jnp.int32) + (gx <= size_x - 2).astype(jnp.int32)
    sides_y = 1 + (gy >= 1).astype(jnp.int32) + (gy <= size_y - 2).astype(jnp.int32)
    for load in loads[0:2]:
        load.wait()
    pl.semaphore_wait(barrier, sides_x * sides_y - 1)
    coarse_a.start()
    for load in loads[2:4]:
        load.wait()
    fine_a.start()
    for load in loads[4:]:
        load.start()
    half = vertical_table12(layers)
    table[...] = jnp.concatenate([half, half], axis=0)

    for n, (dx, dy) in enumerate(DIRS):

        @pl.when(jnp.logical_not(exists(-dx, -dy)))
        def _():
            for exchange in exchanges:
                buffer, where, shape = exchange.targets[n]
                buffer[where] = jnp.zeros(shape, f32)

    cells = (nxc + 4) * span

    def build_mix():
        width = nyc + 4
        reciprocal = (2048 + width - 1) // width
        planes = max(1, 32 // nyf)
        rows = planes * nyf
        cell = lax.broadcasted_iota(jnp.int32, (rows, cells), 1)
        for part in range(nxf // planes):
            here = slice(part * planes, (part + 1) * planes)
            index = index_in[here].reshape(rows, -1)
            weight = weight_in[here].reshape(rows, -1)
            row = jnp.right_shift(index * reciprocal, 11)
            column = index - row * width + (OFF - 2)
            column = jnp.where(column >= span, column - span, column)
            place = row * span + column
            total = jnp.zeros((rows, cells), f32)
            for j in range(index.shape[1]):
                total += jnp.where(cell == place[:, j : j + 1], weight[:, j : j + 1], 0.0)
            mix_high, mix_low = halves(total)
            mix[0, part * rows : (part + 1) * rows] = mix_high
            mix[1, part * rows : (part + 1) * rows] = mix_low

    lane = lax.broadcasted_iota(jnp.int32, (1, 1, layers), 2)

    def tops(parts):
        out = None
        for c, values in enumerate(parts):
            only = jnp.where(lane == layers - 1, values, 0.0)
            moved = pltpu.roll(only.reshape(-1, layers), c + 1, 1).reshape(values.shape)
            out = moved if out is None else out + moved
        return out

    def interface(top, parts):
        high, low = halves(top.reshape(cells, layers))
        found = dot(mix[0], high) + (dot(mix[1], high) + dot(mix[0], low))
        result = []
        for c, values in enumerate(parts):
            moved = found if c == 0 else pltpu.roll(found, layers - c, 1)
            result.append(jnp.where(lane == 0, moved.reshape(values.shape), values))
        return result

    f_in = (slice(2, 2 + nxf), slice(OFF, OFF + nyf))
    c_in = (slice(2, 2 + nxc), slice(OFF, OFF + nyc))

    def parameters(par):
        scale = (time_step * time_step) / par[0]
        shear = par[1]
        par[0] = shear * scale
        par[1] = (par[2] + shear) * scale

    def fine_before(u, earlier):
        before_halo(u, f1.at[3], f_lift, f_base, earlier, f_par.at[0], table[...], nxf, nyf)

    def coarse_before(u, earlier):
        before_halo(u, c1.at[3], c_lift, c_base, earlier, c_par.at[0], table[...], nxc, nyc)

    def fine_after(u, put):
        after_halo(
            u, f1.at[3], f_lift, f_bend, f_base, f_par.at[0], f_par.at[1], table[...], nxf, nyf, 1.0, put
        )

    def coarse_after(u, put):
        after_halo(
            u, c1.at[3], c_lift, c_bend, c_base, c_par.at[0], c_par.at[1], table[...], nxc, nyc, 2.0, put
        )

    def put_in(buffer, where):
        def put(c, row, values):
            buffer[c, where[0].start + row, where[1]] = values

        return put

    def put_out(buffer):
        def put(c, row, values):
            buffer[c, row] = values

        return put

    for load in loads[4:8]:
        load.wait()
    parameters(c_par)
    coarse_before(c1, lambda c: c_old[c])
    for load in loads[8:12]:
        load.wait()
    parameters(f_par)
    fine_before(f1, lambda c: f_old[c])
    coarse_a.arrive()
    coarse_after(c1, put_in(c2, c_in))
    coarse_b.start()
    fine_a.arrive()
    fine_after(f1, put_in(f2, f_in))
    for load in loads[12:]:
        load.wait()
    build_mix()
    coarse_before(c2, lambda c: c1[c, c_in[0], c_in[1]])
    coarse_a.finish()
    fine_a.finish()
    coarse_b.arrive()
    sub = lax.broadcasted_iota(jnp.int32, (1, OFF, 1), 1)
    rims = []
    for c in range(3):
        after, before = c2[c, :, OFF + nyc : 2 * OFF + nyc], c2[c, :, 0:OFF]
        rims.append(jnp.where(sub < 2, after, jnp.where(sub >= OFF - 2, before, 0.0)))
    top = jnp.concatenate([tops(rims), tops([c2[c, :, c_in[1]] for c in range(3)])], axis=1)
    for c, values in enumerate(interface(top, [f2[c, f_in[0], f_in[1]] for c in range(3)])):
        f2[c, f_in[0], f_in[1]] = values
    fine_b.start()

    coarse_after(c2, put_out(coarse_out))
    t2[c_in[0], c_in[1]] = tops([coarse_out[c] for c in range(3)])
    top_c.start()
    fine_before(f2, lambda c: f1[c, f_in[0], f_in[1]])
    coarse_b.finish()
    fine_b.arrive()
    fine_after(f2, put_out(fine_out))
    fine_b.finish()
    top_c.arrive()
    rim = jnp.where(jnp.logical_or(sub < 2, sub >= OFF - 2), t2[:, 0:OFF], 0.0)
    top = jnp.concatenate([rim, t2[:, OFF:span]], axis=1)
    for c, values in enumerate(interface(top, [fine_out[c] for c in range(3)])):
        fine_out[c] = values
    top_c.finish()


def finish(fine_in, coarse_in, fine_out, coarse_out, sem):
    copies = [
        pltpu.make_async_copy(fine_in, fine_out, sem.at[0]),
        pltpu.make_async_copy(coarse_in, coarse_out, sem.at[1]),
    ]
    for copy in copies:
        copy.start()
    for copy in copies:
        copy.wait()


def solution(mesh):
    size_x, size_y = mesh.shape["gx"], mesh.shape["gy"]

    def on_device(*args):
        fine, coarse = args[0], args[2]
        _, nxf, nyf, layers = fine.shape
        _, nxc, nyc, _ = coarse.shape
        index = args[12]

        def wide(parts, nx, ny):
            return pltpu.VMEM((parts, nx + 4, ny + 2 * OFF, layers), f32)

        span = OFF + nyc
        scratch = [
            wide(4, nxf, nyf),
            wide(3, nxf, nyf),
            wide(4, nxc, nyc),
            wide(3, nxc, nyc),
            pltpu.VMEM(fine.shape, f32),
            pltpu.VMEM(coarse.shape, f32),
            pltpu.VMEM(fine.shape, f32),
            pltpu.VMEM(coarse.shape, f32),
            pltpu.VMEM(index.shape, jnp.int32),
            pltpu.VMEM(index.shape, f32),
            pltpu.VMEM((nxf + 4, nyf + 2 * OFF, layers), f32),
            pltpu.VMEM((nxf, nyf + 2 * OFF, layers), f32),
            pltpu.VMEM((nxc + 4, nyc + 2 * OFF, layers), f32),
            pltpu.VMEM((nxc, nyc + 2 * OFF, layers), f32),
            pltpu.VMEM((nxc + 4, span, layers), f32),
            pltpu.VMEM((2, nxf * nyf, (nxc + 4) * span), bf16),
            pltpu.VMEM((2 * layers, layers), bf16),
            pltpu.VMEM(fine.shape, f32),
            pltpu.VMEM(coarse.shape, f32),
            pltpu.SemaphoreType.DMA((14,)),
            pltpu.SemaphoreType.DMA((40,)),
            pltpu.SemaphoreType.DMA((40,)),
        ]
        shapes = (
            jax.ShapeDtypeStruct(fine.shape, f32),
            jax.ShapeDtypeStruct(coarse.shape, f32),
        )
        hbm, vmem = pl.BlockSpec(memory_space=pltpu.HBM), pl.BlockSpec(memory_space=pltpu.VMEM)
        args = [pltpu.with_memory_space_constraint(arg, pltpu.HBM) for arg in args]
        results = pl.pallas_call(
            functools.partial(kernel, size_x, size_y),
            out_shape=(pltpu.VMEM(fine.shape, f32), pltpu.VMEM(coarse.shape, f32)),
            in_specs=[hbm] * 14,
            out_specs=(vmem, vmem),
            scratch_shapes=scratch,
            compiler_params=pltpu.CompilerParams(
                collective_id=0, has_side_effects=True, vmem_limit_bytes=32 * 1024 * 1024
            ),
        )(*args)
        return pl.pallas_call(
            finish,
            out_shape=shapes,
            in_specs=[vmem, vmem],
            out_specs=(hbm, hbm),
            scratch_shapes=[pltpu.SemaphoreType.DMA((2,))],
            compiler_params=pltpu.CompilerParams(vmem_limit_bytes=16 * 1024 * 1024),
        )(*results)

    field, flat = P(None, "gx", "gy", None), P("gx", "gy", None)
    return jax.shard_map(
        on_device,
        mesh=mesh,
        in_specs=(field,) * 4 + (flat,) * 10,
        out_specs=(field, field),
        check_vma=False,
    )
```

```python
import functools

import jax
import jax.numpy as jnp
from jax import lax
from jax.experimental import pallas as pl
from jax.experimental.pallas import tpu as pltpu
from jax.sharding import PartitionSpec as P

MESH = pl.DeviceIdType.MESH
f32 = jnp.float32
bf16 = jnp.bfloat16
time_step = 0.25
OFF = 8
SIDES = ((-1, 0), (1, 0), (0, -1), (0, 1))
CORNERS = ((-1, -1), (-1, 1), (1, -1), (1, 1))
DIRS = SIDES + CORNERS


def vertical_table12(layers):
    level_in = lax.broadcasted_iota(jnp.int32, (layers, layers), 0)
    level_out = lax.broadcasted_iota(jnp.int32, (layers, layers), 1)
    apart = level_in - level_out
    table = jnp.where(apart == -2, 1.0, 0.0)
    table = jnp.where(apart == -1, -8.0, table)
    table = jnp.where(apart == 1, 8.0, table)
    table = jnp.where(apart == 2, -1.0, table)
    last = layers - 1
    edges = {
        0: ((0, -18.0), (1, 24.0), (2, -6.0)),
        1: ((0, -6.0), (2, 6.0)),
        last - 1: ((last - 2, -6.0), (last, 6.0)),
        last: ((last - 2, 6.0), (last - 1, -24.0), (last, 18.0)),
    }
    for row, taps in edges.items():
        column = jnp.zeros_like(table)
        for level, value in taps:
            column = jnp.where(level_in == level, value, column)
        table = jnp.where(level_out == row, column, table)
    return table.astype(bf16)


def halves(values):
    high = values.astype(bf16)
    low = (values - high.astype(f32)).astype(bf16)
    return high, low


def dot(left, right):
    return jnp.dot(left, right, preferred_element_type=f32)


def vertical12(values, table2):
    shape = values.shape
    high, low = halves(values.reshape(-1, shape[-1]))
    return dot(jnp.concatenate([high, low], axis=1), table2).reshape(shape)


def before_halo(u, metric, lift, base, earlier, shear, table2, nx, ny):
    inner_x, inner_y = slice(2, 2 + nx), slice(OFF, OFF + ny)
    metric_in = metric[inner_x, inner_y] * (1.0 / 12.0)
    slopes = [metric_in * vertical12(u[c, inner_x, inner_y], table2) for c in range(3)]
    lift[inner_x, inner_y] = slopes[2]
    for c in range(3):
        bent = metric_in * vertical12(slopes[c], table2)
        base[c] = 2.0 * u[c, inner_x, inner_y] - earlier(c) + shear[...] * bent


def after_halo(u, metric, lift, bend, base, shear, both, table2, nx, ny, spacing, put):
    inner_x, inner_y = slice(2, 2 + nx), slice(OFF, OFF + ny)
    t1 = 1.0 / (12.0 * spacing)
    t2 = 1.0 / (12.0 * spacing * spacing)
    taps = (-2, -1, 1, 2)

    def first(m2, m1, p1, p2):
        return t1 * (m2 - p2) + (8.0 * t1) * (p1 - m1)

    def pairs(m2, m1, p1, p2):
        return m1 + p1, m2 + p2

    def second(near, far, mid, weight):
        return (16.0 * t2) * near - t2 * far - (weight * t2) * mid

    def shifted(read):
        return [read(slice(OFF + s, OFF + s + ny)) for s in taps]

    layers = u.shape[-1]
    rims = (
        (slice(0, 2), inner_y),
        (slice(2 + nx, 4 + nx), inner_y),
        (inner_x, slice(0, OFF)),
        (inner_x, slice(OFF + ny, 2 * OFF + ny)),
    )
    for xs, ys in rims:
        lift[xs, ys] = (metric[xs, ys] * (1.0 / 12.0)) * vertical12(u[2, xs, ys], table2)

    slants, sums = [], []
    for row in range(nx + 4):
        near_y = shifted(lambda ys: u[1, row, ys])
        slants.append(first(*near_y) + lift[row, inner_y])
        sums.append(pairs(*near_y))
        i = row - 4
        if i < 0:
            continue
        m = i + 2
        wide = [u[0, m + s] for s in taps]
        bend[i] = first(*wide) + lift[m]
        near, far = pairs(*[v[inner_y] for v in wide])
        mid = u[0, m, inner_y]
        curve_x = second(near, far, mid, 30.0)
        near, far = pairs(*shifted(lambda ys: u[0, m, ys]))
        curve = curve_x + second(near, far, mid, 30.0)
        graddiv = curve_x + first(*[slants[m + s] for s in taps])
        put(0, i, base[0, i] + shear[i] * curve + both[i] * graddiv)
        near, far = sums[m]
        mid = u[1, m, inner_y]
        curve_y = second(near, far, mid, 30.0)
        near, far = pairs(*[u[1, m + s, inner_y] for s in taps])
        curve = curve_y + second(near, far, mid, 30.0)
        graddiv = curve_y + first(*shifted(lambda ys: bend[i, ys]))
        put(1, i, base[1, i] + shear[i] * curve + both[i] * graddiv)
        near, far = pairs(*[u[2, m + s, inner_y] for s in taps])
        near_y, far_y = pairs(*shifted(lambda ys: u[2, m, ys]))
        curve = second(near + near_y, far + far_y, u[2, m, inner_y], 60.0)
        base[2, i] = base[2, i] + shear[i] * curve
        base[0, i] = slants[m] + (bend[i, inner_y] - lift[m, inner_y])

    bent = (metric[inner_x, inner_y] * (1.0 / 12.0)) * vertical12(base[0], table2)
    for i in range(nx):
        put(2, i, base[2, i] + both[i] * bent[i])


def kernel(
    size_x,
    size_y,
    fine_now,
    fine_prev,
    coarse_now,
    coarse_prev,
    fine_rho,
    fine_mu,
    fine_lam,
    fine_metric,
    coarse_rho,
    coarse_mu,
    coarse_lam,
    coarse_metric,
    couple_index,
    couple_weight,
    fine_out,
    coarse_out,
    f1,
    f2,
    c1,
    c2,
    f_old,
    c_old,
    f_par,
    c_par,
    index_in,
    weight_in,
    f_lift,
    f_bend,
    c_lift,
    c_bend,
    t2,
    mix,
    table,
    f_base,
    c_base,
    load_sem,
    send_sem,
    recv_sem,
):
    nxf, nyf, layers = fine_rho.shape
    nxc, nyc, _ = coarse_rho.shape
    span = OFF + nyc
    gx, gy = lax.axis_index("gx"), lax.axis_index("gy")

    def inner(nx, ny):
        return pl.ds(2, nx), pl.ds(OFF, ny)

    def exists(dx, dy):
        ok = None
        for step, position, size in ((dx, gx, size_x), (dy, gy, size_y)):
            if step:
                here = position >= 1 if step < 0 else position <= size - 2
                ok = here if ok is None else jnp.logical_and(ok, here)
        return ok

    barrier = pltpu.get_barrier_semaphore()
    for dx, dy in DIRS:

        @pl.when(exists(dx, dy))
        def _():
            pl.semaphore_signal(
                barrier, inc=1, device_id=(gx + dx, gy + dy), device_id_type=MESH
            )

    fx, fy = inner(nxf, nyf)
    cx, cy = inner(nxc, nyc)
    pairs = [
        (coarse_now, c1.at[0:3, cx, cy]),
        (coarse_metric, c1.at[3, cx, cy]),
        (fine_now, f1.at[0:3, fx, fy]),
        (fine_metric, f1.at[3, fx, fy]),
        (coarse_rho, c_par.at[0]),
        (coarse_mu, c_par.at[1]),
        (coarse_lam, c_par.at[2]),
        (coarse_prev, c_old),
        (fine_rho, f_par.at[0]),
        (fine_mu, f_par.at[1]),
        (fine_lam, f_par.at[2]),
        (fine_prev, f_old),
        (couple_index, index_in),
        (couple_weight, weight_in),
    ]
    loads = [
        pltpu.make_async_copy(source, target, load_sem.at[n])
        for n, (source, target) in enumerate(pairs)
    ]
    for load in loads[0:4]:
        load.start()

    def source_range(step, start, length):
        return {-1: pl.ds(start, 2), 1: pl.ds(start + length - 2, 2), 0: pl.ds(start, length)}[step]

    def target_range(step, start, length, wrap=0):
        after = start + length - wrap
        return {-1: pl.ds(after, 2), 1: pl.ds(start - 2, 2), 0: pl.ds(start, length)}[step]

    class Exchange:
        def __init__(self, base, buffer, nx, ny, sides, corners, wrap=0):
            self.copies = []
            self.targets = []
            for n, (dx, dy) in enumerate(DIRS):
                parts = sides if n < 4 else corners
                xs, ys = source_range(dx, 2, nx), source_range(dy, OFF, ny)
                xt, yt = target_range(dx, 2, nx), target_range(dy, OFF, ny, wrap)
                if parts is None:
                    src, dst = buffer.at[xs, ys], buffer.at[xt, yt]
                    self.targets.append((buffer, (xt, yt), (xt.size, yt.size, layers)))
                else:
                    ps = pl.ds(0, parts)
                    src, dst = buffer.at[ps, xs, ys], buffer.at[ps, xt, yt]
                    self.targets.append((buffer, (ps, xt, yt), (parts, xt.size, yt.size, layers)))
                copy = pltpu.make_async_remote_copy(
                    src_ref=src,
                    dst_ref=dst,
                    send_sem=send_sem.at[base + n],
                    recv_sem=recv_sem.at[base + n],
                    device_id=(gx + dx, gy + dy),
                    device_id_type=MESH,
                )
                self.copies.append(copy)

        def start(self):
            for n in (0, 1, 2, 3, 4, 5, 6, 7):
                pl.when(exists(*DIRS[n]))(self.copies[n].start)

        def arrive(self):
            for (dx, dy), copy in zip(DIRS, self.copies):
                pl.when(exists(-dx, -dy))(copy.wait_recv)

        def finish(self):
            for (dx, dy), copy in zip(DIRS, self.copies):
                pl.when(exists(dx, dy))(copy.wait_send)

    coarse_a = Exchange(0, c1, nxc, nyc, 4, 2)
    fine_a = Exchange(8, f1, nxf, nyf, 4, 2)
    coarse_b = Exchange(16, c2, nxc, nyc, 3, 3)
    fine_b = Exchange(24, f2, nxf, nyf, 3, 2)
    top_c = Exchange(32, t2, nxc, nyc, None, None, wrap=span)
    exchanges = (coarse_a, fine_a, coarse_b, fine_b, top_c)

    sides_x = 1 + (gx >= 1).astype(jnp.int32) + (gx <= size_x - 2).astype(jnp.int32)
    sides_y = 1 + (gy >= 1).astype(jnp.int32) + (gy <= size_y - 2).astype(jnp.int32)
    for load in loads[0:2]:
        load.wait()
    pl.semaphore_wait(barrier, sides_x * sides_y - 1)
    coarse_a.start()
    for load in loads[2:4]:
        load.wait()
    fine_a.start()
    for load in loads[4:]:
        load.start()
    half = vertical_table12(layers)
    table[...] = jnp.concatenate([half, half], axis=0)

    for n, (dx, dy) in enumerate(DIRS):

        @pl.when(jnp.logical_not(exists(-dx, -dy)))
        def _():
            for exchange in exchanges:
                buffer, where, shape = exchange.targets[n]
                buffer[where] = jnp.zeros(shape, f32)

    cells = (nxc + 4) * span

    def build_mix():
        width = nyc + 4
        reciprocal = (2048 + width - 1) // width
        planes = max(1, 32 // nyf)
        rows = planes * nyf
        cell = lax.broadcasted_iota(jnp.int32, (rows, cells), 1)
        for part in range(nxf // planes):
            here = slice(part * planes, (part + 1) * planes)
            index = index_in[here].reshape(rows, -1)
            weight = weight_in[here].reshape(rows, -1)
            row = jnp.right_shift(index * reciprocal, 11)
            column = index - row * width + (OFF - 2)
            column = jnp.where(column >= span, column - span, column)
            place = row * span + column
            total = jnp.zeros((rows, cells), f32)
            for j in range(index.shape[1]):
                total += jnp.where(cell == place[:, j : j + 1], weight[:, j : j + 1], 0.0)
            mix_high, mix_low = halves(total)
            mix[0, part * rows : (part + 1) * rows] = mix_high
            mix[1, part * rows : (part + 1) * rows] = mix_low

    lane = lax.broadcasted_iota(jnp.int32, (1, 1, layers), 2)

    def tops(parts):
        out = None
        for c, values in enumerate(parts):
            only = jnp.where(lane == layers - 1, values, 0.0)
            moved = pltpu.roll(only.reshape(-1, layers), c + 1, 1).reshape(values.shape)
            out = moved if out is None else out + moved
        return out

    def interface(top, parts):
        high, low = halves(top.reshape(cells, layers))
        found = dot(mix[0], high) + (dot(mix[1], high) + dot(mix[0], low))
        result = []
        for c, values in enumerate(parts):
            moved = found if c == 0 else pltpu.roll(found, layers - c, 1)
            result.append(jnp.where(lane == 0, moved.reshape(values.shape), values))
        return result

    f_in = (slice(2, 2 + nxf), slice(OFF, OFF + nyf))
    c_in = (slice(2, 2 + nxc), slice(OFF, OFF + nyc))

    def parameters(par):
        scale = (time_step * time_step) / par[0]
        shear = par[1]
        par[0] = shear * scale
        par[1] = (par[2] + shear) * scale

    def fine_before(u, earlier):
        before_halo(u, f1.at[3], f_lift, f_base, earlier, f_par.at[0], table[...], nxf, nyf)

    def coarse_before(u, earlier):
        before_halo(u, c1.at[3], c_lift, c_base, earlier, c_par.at[0], table[...], nxc, nyc)

    def fine_after(u, put):
        after_halo(
            u, f1.at[3], f_lift, f_bend, f_base, f_par.at[0], f_par.at[1], table[...], nxf, nyf, 1.0, put
        )

    def coarse_after(u, put):
        after_halo(
            u, c1.at[3], c_lift, c_bend, c_base, c_par.at[0], c_par.at[1], table[...], nxc, nyc, 2.0, put
        )

    def put_in(buffer, where):
        def put(c, row, values):
            buffer[c, where[0].start + row, where[1]] = values

        return put

    def put_out(buffer):
        def put(c, row, values):
            buffer[c, row] = values

        return put

    for load in loads[4:8]:
        load.wait()
    parameters(c_par)
    coarse_before(c1, lambda c: c_old[c])
    for load in loads[8:12]:
        load.wait()
    parameters(f_par)
    fine_before(f1, lambda c: f_old[c])
    coarse_a.arrive()
    coarse_after(c1, put_in(c2, c_in))
    coarse_b.start()
    fine_a.arrive()
    fine_after(f1, put_in(f2, f_in))
    for load in loads[12:]:
        load.wait()
    build_mix()
    coarse_before(c2, lambda c: c1[c, c_in[0], c_in[1]])
    coarse_a.finish()
    fine_a.finish()
    coarse_b.arrive()
    sub = lax.broadcasted_iota(jnp.int32, (1, OFF, 1), 1)
    rims = []
    for c in range(3):
        after, before = c2[c, :, OFF + nyc : 2 * OFF + nyc], c2[c, :, 0:OFF]
        rims.append(jnp.where(sub < 2, after, jnp.where(sub >= OFF - 2, before, 0.0)))
    top = jnp.concatenate([tops(rims), tops([c2[c, :, c_in[1]] for c in range(3)])], axis=1)
    for c, values in enumerate(interface(top, [f2[c, f_in[0], f_in[1]] for c in range(3)])):
        f2[c, f_in[0], f_in[1]] = values
    fine_b.start()

    coarse_after(c2, put_out(coarse_out))
    t2[c_in[0], c_in[1]] = tops([coarse_out[c] for c in range(3)])
    top_c.start()
    fine_before(f2, lambda c: f1[c, f_in[0], f_in[1]])
    coarse_b.finish()
    fine_b.arrive()
    fine_after(f2, put_out(fine_out))
    fine_b.finish()
    top_c.arrive()
    rim = jnp.where(jnp.logical_or(sub < 2, sub >= OFF - 2), t2[:, 0:OFF], 0.0)
    top = jnp.concatenate([rim, t2[:, OFF:span]], axis=1)
    for c, values in enumerate(interface(top, [fine_out[c] for c in range(3)])):
        fine_out[c] = values
    top_c.finish()


def finish(fine_in, coarse_in, fine_out, coarse_out, sem):
    copies = [
        pltpu.make_async_copy(fine_in, fine_out, sem.at[0]),
        pltpu.make_async_copy(coarse_in, coarse_out, sem.at[1]),
    ]
    for copy in copies:
        copy.start()
    for copy in copies:
        copy.wait()


def solution(mesh):
    size_x, size_y = mesh.shape["gx"], mesh.shape["gy"]

    def on_device(*args):
        fine, coarse = args[0], args[2]
        _, nxf, nyf, layers = fine.shape
        _, nxc, nyc, _ = coarse.shape
        index = args[12]

        def wide(parts, nx, ny):
            return pltpu.VMEM((parts, nx + 4, ny + 2 * OFF, layers), f32)

        span = OFF + nyc
        scratch = [
            wide(4, nxf, nyf),
            wide(3, nxf, nyf),
            wide(4, nxc, nyc),
            wide(3, nxc, nyc),
            pltpu.VMEM(fine.shape, f32),
            pltpu.VMEM(coarse.shape, f32),
            pltpu.VMEM(fine.shape, f32),
            pltpu.VMEM(coarse.shape, f32),
            pltpu.VMEM(index.shape, jnp.int32),
            pltpu.VMEM(index.shape, f32),
            pltpu.VMEM((nxf + 4, nyf + 2 * OFF, layers), f32),
            pltpu.VMEM((nxf, nyf + 2 * OFF, layers), f32),
            pltpu.VMEM((nxc + 4, nyc + 2 * OFF, layers), f32),
            pltpu.VMEM((nxc, nyc + 2 * OFF, layers), f32),
            pltpu.VMEM((nxc + 4, span, layers), f32),
            pltpu.VMEM((2, nxf * nyf, (nxc + 4) * span), bf16),
            pltpu.VMEM((2 * layers, layers), bf16),
            pltpu.VMEM(fine.shape, f32),
            pltpu.VMEM(coarse.shape, f32),
            pltpu.SemaphoreType.DMA((14,)),
            pltpu.SemaphoreType.DMA((40,)),
            pltpu.SemaphoreType.DMA((40,)),
        ]
        shapes = (
            jax.ShapeDtypeStruct(fine.shape, f32),
            jax.ShapeDtypeStruct(coarse.shape, f32),
        )
        hbm, vmem = pl.BlockSpec(memory_space=pltpu.HBM), pl.BlockSpec(memory_space=pltpu.VMEM)
        args = [pltpu.with_memory_space_constraint(arg, pltpu.HBM) for arg in args]
        results = pl.pallas_call(
            functools.partial(kernel, size_x, size_y),
            out_shape=(pltpu.VMEM(fine.shape, f32), pltpu.VMEM(coarse.shape, f32)),
            in_specs=[hbm] * 14,
            out_specs=(vmem, vmem),
            scratch_shapes=scratch,
            compiler_params=pltpu.CompilerParams(
                collective_id=0, has_side_effects=True, vmem_limit_bytes=32 * 1024 * 1024
            ),
        )(*args)
        return pl.pallas_call(
            finish,
            out_shape=shapes,
            in_specs=[vmem, vmem],
            out_specs=(hbm, hbm),
            scratch_shapes=[pltpu.SemaphoreType.DMA((2,))],
            compiler_params=pltpu.CompilerParams(vmem_limit_bytes=16 * 1024 * 1024),
        )(*results)

    field, flat = P(None, "gx", "gy", None), P("gx", "gy", None)
    return jax.shard_map(
        on_device,
        mesh=mesh,
        in_specs=(field,) * 4 + (flat,) * 10,
        out_specs=(field, field),
        check_vma=False,
    )
```
